32 devices in a mesh: store: 8 (over z, y), tp: 4 (over x, core).
Axes of the slice: x: 2, y: 2, z: 4, core: 2. Of those that a mesh axis runs over, the one named last changes fastest.
Arguments:
- queries: bfloat16 [8192, 8192], P('store', 'tp')
- fresh_kv: bfloat16 [2, 8192, 1024], P(None, ('store', 'tp'))
- page_pool: bfloat16 [512, 2, 128, 1024], P('store', None, None, 'tp')
- page_host: int32 [32, 8], P('store'), may hold values from 0 to 7, as said below
- page_slot: int32 [32, 8], P('store'), may hold values from 0 to 63, as said below
- prefix_len: int32 [32], P('store'), may hold values from 513 to 1024
- fresh_len: int32 [8, 4], P('store'), may hold values from 1 to 384, 1024 in all within a row
Outputs:
- attention: bfloat16 [8192, 8192], P('store', 'tp')
The draws below stay inside these ranges and needn't reach their ends.
Inputs may be any that keep to these rules, and one draw needn't show every extreme that they name: `page_host`: page p of request r is read only if p < ceil(prefix_len[r] / 128). Among the pages read by the 4 requests of one host, at most 4 lie on any one host; in every draw some host holds exactly 4 of the pages read by each host. `page_slot`: several entries may name the same stored page. `fresh_len`: the requests of a host own consecutive rows of its block, in order.
All inputs are finite; a program needn't handle non-finite values.
Results may differ from the reference program's by a relative error of at most 0.0041.
Values may be sent and summed in bfloat16 or wider, within the bound.
No kernel may reach another device: no remote copies, remote signals or barrier semaphores. Data moves between devices by JAX's collectives and lax.ppermute only.
A program may use at most 128 MiB of HBM per device.

```python
import math
import jax
import jax.numpy as jnp
import numpy as np
from jax import lax

QH = 64
KVH = 8
HD = 128
TOK_HOST = 1024
REQ_HOST = 4
PAGE = 128
PAGES_MAX = 8
SLOTS = 64
MOST_NEW = 384
CAP = 4
TOKENS = 8192
REQS = 32
N_STORE = 8


def host_table(host_key, host_id, hot_host):
    subkeys = jax.random.split(host_key, 6)
    entry_count = REQ_HOST * PAGES_MAX
    host_count = REQS // REQ_HOST
    fewest = PAGES_MAX * 5 // 8
    page_count = jax.random.randint(subkeys[0], (REQ_HOST,), fewest, PAGES_MAX + 1)
    filled = jax.random.randint(subkeys[1], (REQ_HOST,), 1, PAGE + 1)
    is_hot = host_id == hot_host
    page_count = page_count.at[0].set(jnp.where(is_hot, PAGES_MAX, page_count[0]))
    filled = filled.at[0].set(jnp.where(is_hot, PAGE, filled[0]))
    page_count = page_count.at[1].set(jnp.where(is_hot, fewest, page_count[1]))
    filled = filled.at[1].set(jnp.where(is_hot, 1, filled[1]))
    prefix = (page_count - 1) * PAGE + filled
    in_use = (jnp.arange(PAGES_MAX)[None, :] < page_count[:, None]).reshape(entry_count)
    shuffle = jax.random.permutation(subkeys[2], entry_count)
    ordering = jnp.argsort(jnp.where(in_use, 0, entry_count) + shuffle)
    entry_rank = jnp.argsort(ordering)
    grid_size = host_count * CAP
    grid_shuffle = jax.random.permutation(subkeys[3], grid_size)
    grid_owner = jnp.arange(grid_size) // CAP
    grid_order = jnp.argsort(jnp.where(grid_owner == hot_host, grid_shuffle - grid_size, grid_shuffle))
    placed = grid_order[jnp.minimum(entry_rank, grid_size - 1)] // CAP
    owners = jnp.where(in_use, placed, jax.random.randint(subkeys[4], (entry_count,), 0, host_count))
    slot_ids = jax.random.randint(subkeys[5], (entry_count,), 0, SLOTS)
    return (owners.reshape(REQ_HOST, PAGES_MAX), slot_ids.reshape(REQ_HOST, PAGES_MAX), prefix)


def page_tables(key):
    base_key = jax.random.fold_in(key, 901)
    host_count = REQS // REQ_HOST
    hot_host = jax.random.randint(jax.random.fold_in(base_key, 1), (), 0, host_count)
    host_keys = jax.random.split(jax.random.fold_in(base_key, 2), host_count)
    owners, slot_ids, prefix = jax.vmap(host_table, in_axes=(0, 0, None))(host_keys, jnp.arange(host_count), hot_host)
    return (owners.reshape(REQS, PAGES_MAX).astype(jnp.int32), slot_ids.reshape(REQS, PAGES_MAX).astype(jnp.int32), prefix.reshape(REQS).astype(jnp.int32))


def draw_page_host(key, part):
    return page_tables(key)[0]


def draw_page_slot(key, part):
    return page_tables(key)[1]


def draw_prefix_len(key, part):
    return page_tables(key)[2]


def draw_queries(key, part):
    values = jnp.clip(jax.random.normal(jax.random.fold_in(key, 911), (TOKENS, QH * HD), jnp.float32), -6.0, 6.0)
    values = values * 1.5
    return values.astype(jnp.bfloat16)


def draw_fresh_kv(key, part):
    values = jnp.clip(jax.random.normal(jax.random.fold_in(key, 921), (2, TOKENS, KVH * HD), jnp.float32), -6.0, 6.0)
    return values.astype(jnp.bfloat16)


def draw_page_pool(key, part):
    host_count = REQS // REQ_HOST
    values = jnp.clip(jax.random.normal(jax.random.fold_in(key, 931), (host_count * SLOTS, 2, PAGE, KVH * HD), jnp.float32), -6.0, 6.0)
    return values.astype(jnp.bfloat16)


def split_up(count, total, limit, slope):
    loads = [(1 << 20) // math.isqrt(standing ** slope) + 1 for standing in range(2, count + 1)]
    surplus, holding = total - limit - (count - 1), [1] * (count - 1)
    while surplus > 0:
        candidates = [i for i in range(count - 1) if holding[i] < limit]
        mass, budget = sum([loads[i] for i in candidates]), surplus
        for i in candidates:
            addition = min(limit - holding[i], max(1, budget * loads[i] // mass), surplus)
            holding[i] = holding[i] + addition
            surplus = surplus - addition
    return np.array([limit] + holding)


def uneven(own_key, count, total, most, slope):
    if count == 2:
        one = jax.random.randint(own_key, (), max(1, total - most), min(most, total - 1) + 1)
        return jnp.stack([one, total - one])
    sizes = jnp.asarray(split_up(count, total, most, slope), jnp.int32)
    couples = (count - 1) // 2
    giver, taker = sizes[1:1 + 2 * couples:2], sizes[2:2 + 2 * couples:2]
    margin = jnp.minimum(giver - 1, most - taker)
    moved = jax.random.randint(jax.random.fold_in(own_key, 1), (couples,), 0, 1 << 20) % (margin + 1)
    sizes = sizes.at[1:1 + 2 * couples:2].set(giver - moved).at[2:2 + 2 * couples:2].set(taker + moved)
    return sizes[jax.random.permutation(jax.random.fold_in(own_key, 2), count)]


def setup_inputs(seed: int = 0) -> dict:
    seeds = jax.random.split(jax.random.key(seed), 8)
    queries = draw_queries(jax.random.fold_in(seeds[7], 71), 0)
    fresh_kv = draw_fresh_kv(jax.random.fold_in(seeds[7], 71), 0)
    page_pool = draw_page_pool(jax.random.fold_in(seeds[7], 71), 0)
    page_host = draw_page_host(jax.random.fold_in(seeds[7], 71), 0)
    page_slot = draw_page_slot(jax.random.fold_in(seeds[7], 71), 0)
    prefix_len = draw_prefix_len(jax.random.fold_in(seeds[7], 71), 0)
    fresh_len = jax.vmap(lambda own: uneven(own, REQ_HOST, TOK_HOST, MOST_NEW, 2))(jax.random.split(seeds[6], N_STORE)).reshape((N_STORE, REQ_HOST)).astype(jnp.int32)
    return {"queries": queries, "fresh_kv": fresh_kv, "page_pool": page_pool, "page_host": page_host, "page_slot": page_slot, "prefix_len": prefix_len, "fresh_len": fresh_len}


def request_attention(q_rows, key_rows, value_rows, key_valid):
    scores = jnp.einsum('mkgd,nkd->kgmn', q_rows.astype(jnp.float32), key_rows.astype(jnp.float32)) * (1.0 / math.sqrt(HD))
    row_top = lax.optimization_barrier(jnp.max(jnp.where(key_valid, scores, -1e+30), axis=-1, keepdims=True))
    weights = jnp.where(key_valid, jnp.exp(scores - row_top), 0.0)
    row_total = lax.optimization_barrier(jnp.sum(weights, axis=-1))
    rounded = lax.optimization_barrier(weights.astype(jnp.bfloat16))
    mixed_rows = jnp.einsum('kgmn,nkd->mkgd', rounded.astype(jnp.float32), value_rows.astype(jnp.float32))
    return (mixed_rows / jnp.transpose(row_total, (2, 0, 1))[..., None]).astype(jnp.bfloat16)

def reference(queries, fresh_kv, page_pool, page_host, page_slot, prefix_len, fresh_len):
    group_size = QH // KVH
    offsets = (jnp.cumsum(fresh_len, axis=1) - fresh_len).astype(jnp.int32)
    positions = jnp.arange(MOST_NEW, dtype=jnp.int32)
    cache_index = jnp.arange(PAGES_MAX * PAGE, dtype=jnp.int32)

    def one_request(request_id, output):
        request_id = jnp.asarray(request_id).astype(jnp.int32)
        host_id = (request_id // REQ_HOST).astype(jnp.int32)
        within = (request_id % REQ_HOST).astype(jnp.int32)
        offset = offsets[host_id, within].astype(jnp.int32)
        length = fresh_len[host_id, within].astype(jnp.int32)
        window_start = jnp.minimum(offset, TOK_HOST - MOST_NEW).astype(jnp.int32)
        first_row = (host_id * TOK_HOST + window_start).astype(jnp.int32)
        q_rows = lax.dynamic_slice_in_dim(queries, first_row, MOST_NEW, 0).reshape(MOST_NEW, KVH, group_size, HD)
        new_rows = lax.dynamic_slice_in_dim(fresh_kv, first_row, MOST_NEW, 1).reshape(2, MOST_NEW, KVH, HD)
        page_ids = (page_host[request_id] * SLOTS + page_slot[request_id]).astype(jnp.int32)
        cached = page_pool[page_ids]
        cached_keys = cached[:, 0].reshape(PAGES_MAX * PAGE, KVH, HD)
        cached_values = cached[:, 1].reshape(PAGES_MAX * PAGE, KVH, HD)
        key_rows = jnp.concatenate([cached_keys, new_rows[0]], axis=0)
        value_rows = jnp.concatenate([cached_values, new_rows[1]], axis=0)
        query_pos = window_start + positions
        cache_ok = jnp.broadcast_to(cache_index[None, :] < prefix_len[request_id], (MOST_NEW, PAGES_MAX * PAGE))
        fresh_ok = (query_pos[None, :] >= offset) & (query_pos[None, :] <= query_pos[:, None])
        key_valid = jnp.concatenate([cache_ok, fresh_ok], axis=1)
        mixed_rows = request_attention(q_rows, key_rows, value_rows, key_valid).reshape(MOST_NEW, QH * HD)
        row_ok = (query_pos >= offset) & (query_pos < offset + length)
        old_rows = lax.dynamic_slice_in_dim(output, first_row, MOST_NEW, 0)
        return lax.dynamic_update_slice_in_dim(output, jnp.where(row_ok[:, None], mixed_rows, old_rows), first_row, 0)
    return lax.fori_loop(0, REQS, one_request, jnp.zeros_like(queries))
```

```python
import functools
import math

import jax
import jax.numpy as jnp
from jax import lax
from jax.experimental import pallas as pl
from jax.experimental.pallas import tpu as pltpu
from jax.sharding import PartitionSpec as P

HD = 128
REQ_HOST = 4
PAGE = 128
PAGES_MAX = 8
MOST_NEW = 384
ENTRIES = REQ_HOST * PAGES_MAX

TILE = 64
REACH = 512
CHUNK = 256
SCALE = math.log2(math.e) / math.sqrt(HD)
LOW = -3e38
LIMIT = 2.0**60

ANY = pl.BlockSpec(memory_space=pl.ANY)
SMEM = pl.BlockSpec(memory_space=pltpu.SMEM)
VMEM_LIMIT = 63 * 2**20


def collect_kernel(partners, capacity, slots, pairs, after, *refs):
    n = len(partners)
    refs = list(refs)
    take_refs = lambda count: [refs.pop(0) for _ in range(count)]
    codes, (pool,) = take_refs(pairs), take_refs(1)
    take_refs(after)
    sends = take_refs(n)
    held, chosen, sems = refs
    me = lax.axis_index("store")

    def take(i, rank, slot):
        return pltpu.make_async_copy(pool.at[slot], held.at[i, rank], sems.at[0, i, rank])

    def give(i, rank):
        return pltpu.make_async_copy(held.at[i, rank], sends[i].at[rank], sems.at[1, i, rank])

    for i in range(n):
        for rank in range(capacity):
            chosen[rank] = 0

        table, first_row = codes[partners[i] // 2], REQ_HOST * (partners[i] % 2)

        def scan(entry, found, table=table, first_row=first_row):
            code = table[first_row + entry // PAGES_MAX, entry % PAGES_MAX] - me * slots
            hit = (code >= 0) & (code < slots)
            chosen[found] = jnp.where(hit, code, 0)
            return found + hit.astype(jnp.int32)

        lax.fori_loop(0, ENTRIES, scan, jnp.int32(0), unroll=8)
        for rank in range(capacity):
            take(i, rank, chosen[rank]).start()
    for i in range(n):
        for rank in range(capacity):
            take(i, rank, 0).wait()
            give(i, rank).start()
    for i in range(n):
        for rank in range(capacity):
            give(i, rank).wait()


def collect(partners, capacity, codes, pool, after):
    shape = jax.ShapeDtypeStruct((capacity,) + pool.shape[1:], pool.dtype)
    n = len(partners)
    return pl.pallas_call(
        functools.partial(collect_kernel, partners, capacity, pool.shape[0], len(codes), len(after)),
        out_shape=[shape] * n,
        in_specs=[SMEM] * len(codes) + [ANY] * (1 + len(after)),
        out_specs=[ANY] * n,
        scratch_shapes=[
            pltpu.VMEM((n, capacity) + pool.shape[1:], pool.dtype),
            pltpu.SMEM((capacity + 2,), jnp.int32),
            pltpu.SemaphoreType.DMA((2, n, capacity)),
        ],
        compiler_params=pltpu.CompilerParams(vmem_limit_bytes=VMEM_LIMIT),
        cost_estimate=pl.CostEstimate(
            flops=0,
            bytes_accessed=2 * n * capacity * math.prod(pool.shape[1:]) * 2,
            transcendentals=0,
        ),
        name="collect",
    )(*codes, pool, *after)


def stage_kernel(plan, *refs):
    partners, first, last = plan["partners"], plan["first"], plan["last"]
    blocks, heads, kv_heads = plan["rows"], plan["heads"], plan["kv_heads"]
    group = heads // kv_heads
    refs = list(refs)
    take = lambda n: [refs.pop(0) for _ in range(n)]
    codes, prefix, lengths, queries = take(4)
    pages = take(len(partners))
    pieces = take(plan["pieces"]) if first else []
    if not first:
        (state_in,) = take(1)
    take(plan["carried"])
    (result,) = take(1)
    take(plan["carried"])
    q, state, kv, flipped, peak, info, count, valid, counters, page_sems, row_sems, state_sems = take(12)
    if first:
        fresh, fresh_flipped, fresh_sems = take(3)
    if last:
        outs, out_sems = take(2)
    me = lax.axis_index("store")
    n_chunks = blocks // CHUNK

    def row_copy(c):
        span = pl.ds(pl.multiple_of(c * CHUNK, CHUNK), CHUNK)
        return pltpu.make_async_copy(queries.at[span], q.at[span], row_sems.at[c])

    offset, base = jnp.int32(0), jnp.int32(0)
    for request in range(REQ_HOST):
        end = offset + lengths[0, request]
        begin_row = (offset // 16) * 16
        tiles = (end - begin_row + TILE - 1) // TILE
        for i, value in enumerate((offset, end, begin_row, tiles, base)):
            info[request, i] = value
        offset, base = end, base + tiles
        count[request] = 0
    for owner in range(plan["stores"]):
        counters[owner] = 0

    def fetch(entry, carry):
        request, page = entry // PAGES_MAX, entry % PAGES_MAX
        code = codes[request, page]
        used = code >= 0
        code = jnp.maximum(code, 0)
        owner, slot = lax.div(code, plan["slots"]), lax.rem(code, plan["slots"])
        rank = counters[owner]
        counters[owner] = rank + used.astype(jnp.int32)
        place = count[request]
        here = jnp.bool_(False)
        for i, partner in enumerate(partners):
            mine = used & (owner == lax.bitwise_xor(me, jnp.int32(partner)))
            index = slot if partner == 0 else rank

            @pl.when(mine)
            def _(i=i, index=index):
                span = pl.ds(pl.multiple_of(place * PAGE, PAGE), PAGE)
                pltpu.make_async_copy(
                    pages[i].at[index], kv.at[request, :, span], page_sems.at[request, place]
                ).start()

            here = here | mine

        @pl.when(here)
        def _():
            valid[request, place] = jnp.minimum(prefix[request] - page * PAGE, PAGE)
            count[request] = place + 1

        return carry

    if first:
        tp_me = lax.axis_index("tp")
        piece_copies = []
        for i in range(len(pieces)):
            n = pieces[i].shape[1]
            span = pl.ds(pl.multiple_of(lax.bitwise_xor(tp_me, jnp.int32(i)) * n, n), n)
            piece_copies.append(pltpu.make_async_copy(pieces[i], fresh.at[:, span], fresh_sems.at[i]))
            piece_copies[-1].start()
        rest = pl.ds(blocks, REACH)
        fresh[0, rest, :] = jnp.zeros((REACH, fresh.shape[2]), fresh.dtype)
        fresh_flipped[:, :, rest] = jnp.zeros((kv_heads, HD + 16, REACH), fresh.dtype)
    for c in range(n_chunks):
        row_copy(c).start()
    lax.fori_loop(0, ENTRIES, fetch, 0)

    if not first:

        def state_copy(v):
            return pltpu.make_async_copy(state_in.at[v], state.at[0, v], state_sems.at[v])

        def load(request, carry):
            needed = info[request, 3] if last else jnp.where(count[request] > 0, info[request, 3], 0)

            def load_one(i, carry):
                state_copy(info[request, 4] + i).start()
                return carry

            return lax.fori_loop(0, needed, load_one, carry)

        lax.fori_loop(0, REQ_HOST, load, 0)

    part = group // 2
    width = part * TILE
    chains = [(h, c) for h in range(kv_heads) for c in range(2)]

    def flip(values, ones, target, span):
        for h in range(kv_heads):
            part = values[:, h * HD : (h + 1) * HD]
            target[h, 0:HD, span] = jnp.transpose(part).astype(jnp.bfloat16)
            target[h, HD : HD + 16, span] = ones.astype(jnp.bfloat16)

    if first:
        for copy in piece_copies:
            copy.wait()

        def flip_fresh(c, carry):
            span = pl.ds(pl.multiple_of(c * PAGE, PAGE), PAGE)
            flip(
                fresh[1, span, :].astype(jnp.float32),
                jnp.ones((16, PAGE), jnp.float32),
                fresh_flipped,
                span,
            )
            return carry

        lax.fori_loop(0, blocks // PAGE, flip_fresh, 0)

    def step(visit, row0, source, owned, key_of, value_of, ok, follow):
        begin = ok is not None
        rows = pl.ds(row0, TILE)

        def score(h, c):
            first_head = h * group + c * part
            stacked = jnp.concatenate(
                [q[rows, pl.ds((first_head + g) * HD, HD)] for g in range(part)], axis=0
            )
            scores = lax.dot_general(
                key_of(h), stacked, (((1,), (1,)), ((), ())), preferred_element_type=jnp.float32
            )
            if begin:
                blocks_of = [scores[:, i : i + PAGE] for i in range(0, width, PAGE)]
                scores = jnp.concatenate([jnp.where(ok, x, LOW) for x in blocks_of], axis=1)
            return scores

        def mix(h, c, scores):
            lanes = pl.ds(c * width, width)
            if not begin:
                top = old_top = state[source, visit, h, HD + 8 : HD + 9, lanes]
            if begin or follow:
                top = jnp.max(scores, axis=0, keepdims=True)
            if follow and not begin:
                top = jnp.maximum(top, old_top)
            weights = jnp.exp2((scores - top) * SCALE).astype(jnp.bfloat16)
            mixed = jnp.dot(value_of(h), weights, preferred_element_type=jnp.float32)[: HD + 8]
            if not begin:
                old = state[source, visit, h, 0 : HD + 8, lanes]
                if follow:
                    old = old * jnp.exp2((old_top - top) * SCALE)
                mixed = old + mixed
            state[1, visit, h, 0 : HD + 8, lanes] = mixed
            state[1, visit, h, HD + 8 : HD + 16, lanes] = jnp.broadcast_to(top, (8, width))
            if not begin and not follow:
                peak[...] = jnp.maximum(peak[...], jnp.where(owned, mixed[HD : HD + 8], 0.0))

        scores = score(*chains[0])
        for i, chain in enumerate(chains):
            ahead = score(*chains[i + 1]) if i + 1 < len(chains) else None
            mix(*chain, scores)
            scores = ahead

    def visits_of(request):
        tiles = info[request, 3]
        return tiles if first or last else jnp.where(count[request] > 0, tiles, 0)

    def arrival(request, ready_rows):
        end_row = info[request, 2] + visits_of(request) * TILE
        need = jnp.minimum((end_row + CHUNK - 1) // CHUNK, n_chunks)

        def arrive(c, carry):
            row_copy(c).wait()
            return carry

        lax.fori_loop(ready_rows, need, arrive, 0)
        return jnp.maximum(ready_rows, need)

    def page_arrival(request):
        def page_arrive(place, carry):
            span = pl.ds(pl.multiple_of(place * PAGE, PAGE), PAGE)
            pltpu.make_async_copy(
                pages[0].at[0], kv.at[request, :, span], page_sems.at[request, place]
            ).wait()
            here = valid[request, place]
            token = lax.broadcasted_iota(jnp.int32, (PAGE, 1), 0)

            @pl.when(here < PAGE)
            def _():
                keys = kv[request, 0, span, :].astype(jnp.float32)
                kv[request, 0, span, :] = jnp.where(token < here, keys, keys[0:1, :]).astype(kv.dtype)

            values = kv[request, 1, span, :].astype(jnp.float32)
            ones = (lax.broadcasted_iota(jnp.int32, (16, PAGE), 1) < here).astype(jnp.float32)
            flip(jnp.where(token < here, values, 0.0), ones, flipped.at[request], span)
            return carry

        lax.fori_loop(0, count[request], page_arrive, 0)

    def state_out(visit):
        return pltpu.make_async_copy(state.at[1, visit], result.at[visit], row_sems.at[n_chunks])

    def work(request, follow):
        offset, end, begin_row, _, base = [info[request, i] for i in range(5)]
        begin_row = pl.multiple_of(begin_row, 16)
        n = count[request]

        def tile(i, carry):
            visit = base + i
            row0 = pl.multiple_of(begin_row + i * TILE, 16)
            position = row0 + lax.rem(lax.broadcasted_iota(jnp.int32, (1, width), 1), TILE)
            owned = (position >= offset) & (position < end)

            def page_step(place, pages_now):
                span = pl.ds(pl.multiple_of(place * PAGE, PAGE), pages_now * PAGE)
                step(
                    visit,
                    row0,
                    1 if first else jnp.minimum(place, 1),
                    owned,
                    lambda h: kv[request, 0, span, pl.ds(h * HD, HD)],
                    lambda h: flipped[request, h, :, span],
                    None,
                    follow,
                )

            if first:
                key0 = pl.multiple_of((offset // PAGE) * PAGE, PAGE)

                def fresh_step(reach):
                    span = pl.ds(key0, reach)
                    key = key0 + lax.broadcasted_iota(jnp.int32, (reach, PAGE), 0)
                    key = jnp.where(key >= offset, key, blocks + REACH)
                    lane = lax.broadcasted_iota(jnp.int32, (reach, PAGE), 1)
                    step(
                        visit,
                        row0,
                        1,
                        owned,
                        lambda h: fresh[0, span, pl.ds(h * HD, HD)],
                        lambda h: fresh_flipped[h, :, span],
                        key <= row0 + lane % TILE,
                        follow,
                    )

                near = row0 + TILE - key0 <= REACH // 2

                @pl.when(near)
                def _():
                    fresh_step(REACH // 2)

                @pl.when(jnp.logical_not(near))
                def _():
                    fresh_step(REACH)

            elif not follow:
                state_copy(visit).wait()

            def four(j, carry):
                page_step(4 * j, 4)
                return carry

            lax.fori_loop(0, n // 4, four, 0)

            @pl.when(n % 4 >= 2)
            def _():
                page_step((n // 4) * 4, 2)

            @pl.when(n % 2 == 1)
            def _():
                page_step(n - 1, 1)

            if last:
                now = jnp.minimum(n, 1)
                top_rows = pl.ds(row0, 16)
                position = row0 + lax.broadcasted_iota(jnp.int32, (16, 1), 0)
                for h in range(kv_heads):
                    share = state[now, visit, h, 0:HD, :]
                    share = share * (1.0 / state[now, visit, h, HD : HD + 1, :])
                    share = jnp.transpose(share)
                    for g in range(group):
                        columns = pl.ds((h * group + g) * HD, HD)
                        rows = share[g * TILE : (g + 1) * TILE]
                        old = outs[top_rows, columns].astype(jnp.float32)
                        outs[top_rows, columns] = jnp.where(
                            position >= offset, rows[:16], old
                        ).astype(outs.dtype)
                        outs[pl.ds(row0 + 16, TILE - 16), columns] = rows[16:].astype(outs.dtype)
            else:
                state_out(visit).start()
            return carry

        lax.fori_loop(0, visits_of(request), tile, 0)

    def out_copy(c):
        span = pl.ds(pl.multiple_of(c * CHUNK, CHUNK), CHUNK)
        return pltpu.make_async_copy(outs.at[span], result.at[span], out_sems.at[c])

    def run(follow):
        def one_request(request, ready):
            ready_rows, ready_out = ready
            if not follow:
                ready_rows = arrival(request, ready_rows)
                page_arrival(request)
            work(request, follow)
            if last:
                done = info[request, 1] // 16 * 16 // CHUNK

                def send(c, carry):
                    out_copy(c).start()
                    return carry

                lax.fori_loop(ready_out, done, send, 0)
                ready_out = done
            return (ready_rows, ready_out)

        ready, _ = lax.fori_loop(0, REQ_HOST, one_request, (jnp.int32(0), jnp.int32(0)))
        if not follow:

            def drain(c, carry):
                row_copy(c).wait()
                return carry

            lax.fori_loop(ready, n_chunks, drain, 0)
        if last:
            for c in range(n_chunks):
                out_copy(c).wait()
        else:

            def stored(request, carry):
                def stored_one(i, carry):
                    state_out(0).wait()
                    return carry

                return lax.fori_loop(0, visits_of(request), stored_one, carry)

            lax.fori_loop(0, REQ_HOST, stored, 0)

    peak[...] = jnp.zeros_like(peak)
    run(False)

    @pl.when(jnp.logical_not(jnp.max(peak[...]) <= LIMIT))
    def _():
        run(True)


def stage(partners, stores, slots, tables, queries, pages, pieces, state, last, carried=()):
    rows, width = queries.shape
    kv_width = pages[0].shape[3]
    first = state is None
    heads, kv_heads = width // HD, kv_width // HD
    plan = dict(
        partners=partners,
        stores=stores,
        slots=slots,
        first=first,
        last=last,
        rows=rows,
        heads=heads,
        kv_heads=kv_heads,
        pieces=len(pieces),
        carried=len(carried),
    )
    visits = (rows + REQ_HOST * (15 + TILE - 1)) // TILE
    state_shape = (visits, kv_heads, HD + 16, heads // kv_heads * TILE)
    n_chunks = rows // CHUNK
    scratch = [
        pltpu.VMEM((rows + TILE, width), queries.dtype),
        pltpu.VMEM((2,) + state_shape, jnp.float32),
        pltpu.VMEM((REQ_HOST, 2, PAGES_MAX * PAGE, kv_width), queries.dtype),
        pltpu.VMEM((REQ_HOST, kv_heads, HD + 16, PAGES_MAX * PAGE), queries.dtype),
        pltpu.VMEM((8, heads // kv_heads // 2 * TILE), jnp.float32),
        pltpu.SMEM((REQ_HOST, 5), jnp.int32),
        pltpu.SMEM((REQ_HOST,), jnp.int32),
        pltpu.SMEM((REQ_HOST, PAGES_MAX), jnp.int32),
        pltpu.SMEM((stores,), jnp.int32),
        pltpu.SemaphoreType.DMA((REQ_HOST, PAGES_MAX)),
        pltpu.SemaphoreType.DMA((n_chunks + 1,)),
        pltpu.SemaphoreType.DMA((visits,)),
    ]
    if first:
        scratch += [
            pltpu.VMEM((2, rows + REACH, kv_width), queries.dtype),
            pltpu.VMEM((kv_heads, HD + 16, rows + REACH), queries.dtype),
            pltpu.SemaphoreType.DMA((len(pieces),)),
        ]
    if last:
        scratch += [
            pltpu.VMEM((rows + TILE, width), queries.dtype),
            pltpu.SemaphoreType.DMA((n_chunks,)),
        ]
    operands = list(tables) + [queries] + pages + pieces + ([] if first else [state]) + list(carried)
    n = len(operands) - len(carried)
    aliases = {} if first or last else {n - 1: 0}
    aliases |= {n + i: 1 + i for i in range(len(carried))}
    keys = len(partners) * PAGE + (MOST_NEW if first else 0)
    result, *carried = pl.pallas_call(
        functools.partial(stage_kernel, plan),
        out_shape=[
            jax.ShapeDtypeStruct(queries.shape, queries.dtype)
            if last
            else jax.ShapeDtypeStruct(state_shape, jnp.float32)
        ]
        + [jax.ShapeDtypeStruct(x.shape, x.dtype) for x in carried],
        in_specs=[SMEM] * 3 + [ANY] * (len(operands) - 3),
        out_specs=[ANY] * (1 + len(carried)),
        scratch_shapes=scratch,
        input_output_aliases=aliases,
        compiler_params=pltpu.CompilerParams(vmem_limit_bytes=VMEM_LIMIT),
        cost_estimate=pl.CostEstimate(
            flops=4 * rows * width * keys,
            bytes_accessed=rows * width * 16,
            transcendentals=rows * heads * keys,
        ),
        name="attend",
    )(*operands)
    return result, carried


def swap(values, axis, size, partner):
    return lax.ppermute(values, axis, [(i, i ^ partner) for i in range(size)])


def local(queries, fresh_kv, page_pool, page_host, page_slot, prefix_len, fresh_len):
    stores, tps = lax.axis_size("store"), lax.axis_size("tp")
    slots, head_width = page_pool.shape[0], page_pool.shape[3]
    capacity = max(2, (ENTRIES + stores - 1) // stores)

    partners = list(range(1, stores))
    far = [d for d in partners if d & (stores // 2)]
    near = [d for d in partners if not d & (stores // 2)]
    half = len(far) // 2
    early, late = far[:half], far[half:]

    in_use = jnp.arange(PAGES_MAX, dtype=jnp.int32)[None, :] * PAGE < prefix_len[:, None]
    code = jnp.where(in_use, page_host * slots + page_slot, -1)
    both = jnp.concatenate([code, swap(code, "store", stores, 1)], axis=0)
    codes = [both] + [swap(both, "store", stores, d) for d in range(2, stores, 2)]

    tp_me = lax.axis_index("tp")

    def piece(d):
        return lax.dynamic_slice_in_dim(
            fresh_kv, lax.bitwise_xor(tp_me, jnp.int32(d)) * head_width, head_width, 2
        )

    pieces = [piece(0)] + [swap(piece(d), "tp", tps, d) for d in range(1, tps)]
    sent = collect(early, capacity, codes, page_pool, pieces)
    arrived = {d: swap(pages, "store", stores, d) for d, pages in zip(early, sent)}

    def attend(partners, pages, pieces, state, last, carried):
        tables = (code, prefix_len, fresh_len)
        return stage(
            partners, stores, slots, tables, queries, pages, pieces, state, last, carried
        )

    state, codes = attend([0], [page_pool], pieces, None, False, codes)
    *sent, waiting = collect(near + late, capacity, codes, page_pool, [])
    arrived |= {d: swap(pages, "store", stores, d) for d, pages in zip(near + late, sent)}
    state, (waiting,) = attend(early, [arrived[d] for d in early], [], state, False, [waiting])
    arrived[late[-1]] = swap(waiting, "store", stores, late[-1])
    for part in (near, late[:-1], late[-1:]):
        state, _ = attend(part, [arrived[d] for d in part], [], state, part == late[-1:], [])
    return state


def solution(mesh):
    placed = (
        P("store", "tp"),
        P(None, ("store", "tp"), None),
        P("store", None, None, "tp"),
        P("store", None),
        P("store", None),
        P("store"),
        P("store", None),
    )
    return jax.shard_map(
        local, mesh=mesh, in_specs=placed, out_specs=P("store", "tp"), check_vma=False
    )
```

```python
import functools
import math

import jax
import jax.numpy as jnp
from jax import lax
from jax.experimental import pallas as pl
from jax.experimental.pallas import tpu as pltpu
from jax.sharding import PartitionSpec as P

HD = 128
REQ_HOST = 4
PAGE = 128
PAGES_MAX = 8
MOST_NEW = 384
ENTRIES = REQ_HOST * PAGES_MAX

TILE = 64
REACH = 512
CHUNK = 256
SCALE = math.log2(math.e) / math.sqrt(HD)
LOW = -3e38
LIMIT = 2.0**60

ANY = pl.BlockSpec(memory_space=pl.ANY)
SMEM = pl.BlockSpec(memory_space=pltpu.SMEM)
VMEM_LIMIT = 63 * 2**20


def collect_kernel(partners, capacity, slots, pairs, after, *refs):
    n = len(partners)
    refs = list(refs)
    take_refs = lambda count: [refs.pop(0) for _ in range(count)]
    codes, (pool,) = take_refs(pairs), take_refs(1)
    take_refs(after)
    sends = take_refs(n)
    held, chosen, sems = refs
    me = lax.axis_index("store")

    def take(i, rank, slot):
        return pltpu.make_async_copy(pool.at[slot], held.at[i, rank], sems.at[0, i, rank])

    def give(i, rank):
        return pltpu.make_async_copy(held.at[i, rank], sends[i].at[rank], sems.at[1, i, rank])

    for i in range(n):
        for rank in range(capacity):
            chosen[rank] = 0

        table, first_row = codes[partners[i] // 2], REQ_HOST * (partners[i] % 2)

        def scan(entry, found, table=table, first_row=first_row):
            code = table[first_row + entry // PAGES_MAX, entry % PAGES_MAX] - me * slots
            hit = (code >= 0) & (code < slots)
            chosen[found] = jnp.where(hit, code, 0)
            return found + hit.astype(jnp.int32)

        lax.fori_loop(0, ENTRIES, scan, jnp.int32(0), unroll=8)
        for rank in range(capacity):
            take(i, rank, chosen[rank]).start()
    for i in range(n):
        for rank in range(capacity):
            take(i, rank, 0).wait()
            give(i, rank).start()
    for i in range(n):
        for rank in range(capacity):
            give(i, rank).wait()


def collect(partners, capacity, codes, pool, after):
    shape = jax.ShapeDtypeStruct((capacity,) + pool.shape[1:], pool.dtype)
    n = len(partners)
    return pl.pallas_call(
        functools.partial(collect_kernel, partners, capacity, pool.shape[0], len(codes), len(after)),
        out_shape=[shape] * n,
        in_specs=[SMEM] * len(codes) + [ANY] * (1 + len(after)),
        out_specs=[ANY] * n,
        scratch_shapes=[
            pltpu.VMEM((n, capacity) + pool.shape[1:], pool.dtype),
            pltpu.SMEM((capacity + 2,), jnp.int32),
            pltpu.SemaphoreType.DMA((2, n, capacity)),
        ],
        compiler_params=pltpu.CompilerParams(vmem_limit_bytes=VMEM_LIMIT),
        cost_estimate=pl.CostEstimate(
            flops=0,
            bytes_accessed=2 * n * capacity * math.prod(pool.shape[1:]) * 2,
            transcendentals=0,
        ),
        name="collect",
    )(*codes, pool, *after)


def stage_kernel(plan, *refs):
    partners, first, last = plan["partners"], plan["first"], plan["last"]
    blocks, heads, kv_heads = plan["rows"], plan["heads"], plan["kv_heads"]
    group = heads // kv_heads
    refs = list(refs)
    take = lambda n: [refs.pop(0) for _ in range(n)]
    codes, prefix, lengths, queries = take(4)
    pages = take(len(partners))
    pieces = take(plan["pieces"]) if first else []
    if not first:
        (state_in,) = take(1)
    take(plan["carried"])
    (result,) = take(1)
    take(plan["carried"])
    q, state, kv, flipped, peak, info, count, valid, counters, page_sems, row_sems, state_sems = take(12)
    if first:
        fresh, fresh_flipped, fresh_sems = take(3)
    if last:
        outs, out_sems = take(2)
    me = lax.axis_index("store")
    n_chunks = blocks // CHUNK

    def row_copy(c):
        span = pl.ds(pl.multiple_of(c * CHUNK, CHUNK), CHUNK)
        return pltpu.make_async_copy(queries.at[span], q.at[span], row_sems.at[c])

    offset, base = jnp.int32(0), jnp.int32(0)
    for request in range(REQ_HOST):
        end = offset + lengths[0, request]
        begin_row = (offset // 16) * 16
        tiles = (end - begin_row + TILE - 1) // TILE
        for i, value in enumerate((offset, end, begin_row, tiles, base)):
            info[request, i] = value
        offset, base = end, base + tiles
        count[request] = 0
    for owner in range(plan["stores"]):
        counters[owner] = 0

    def fetch(entry, carry):
        request, page = entry // PAGES_MAX, entry % PAGES_MAX
        code = codes[request, page]
        used = code >= 0
        code = jnp.maximum(code, 0)
        owner, slot = lax.div(code, plan["slots"]), lax.rem(code, plan["slots"])
        rank = counters[owner]
        counters[owner] = rank + used.astype(jnp.int32)
        place = count[request]
        here = jnp.bool_(False)
        for i, partner in enumerate(partners):
            mine = used & (owner == lax.bitwise_xor(me, jnp.int32(partner)))
            index = slot if partner == 0 else rank

            @pl.when(mine)
            def _(i=i, index=index):
                span = pl.ds(pl.multiple_of(place * PAGE, PAGE), PAGE)
                pltpu.make_async_copy(
                    pages[i].at[index], kv.at[request, :, span], page_sems.at[request, place]
                ).start()

            here = here | mine

        @pl.when(here)
        def _():
            valid[request, place] = jnp.minimum(prefix[request] - page * PAGE, PAGE)
            count[request] = place + 1

        return carry

    if first:
        tp_me = lax.axis_index("tp")
        piece_copies = []
        for i in range(len(pieces)):
            n = pieces[i].shape[1]
            span = pl.ds(pl.multiple_of(lax.bitwise_xor(tp_me, jnp.int32(i)) * n, n), n)
            piece_copies.append(pltpu.make_async_copy(pieces[i], fresh.at[:, span], fresh_sems.at[i]))
            piece_copies[-1].start()
        rest = pl.ds(blocks, REACH)
        fresh[0, rest, :] = jnp.zeros((REACH, fresh.shape[2]), fresh.dtype)
        fresh_flipped[:, :, rest] = jnp.zeros((kv_heads, HD + 16, REACH), fresh.dtype)
    for c in range(n_chunks):
        row_copy(c).start()
    lax.fori_loop(0, ENTRIES, fetch, 0)

    if not first:

        def state_copy(v):
            return pltpu.make_async_copy(state_in.at[v], state.at[v], state_sems.at[v])

        def load(request, carry):
            needed = info[request, 3] if last else jnp.where(count[request] > 0, info[request, 3], 0)

            def load_one(i, carry):
                state_copy(info[request, 4] + i).start()
                return carry

            return lax.fori_loop(0, needed, load_one, carry)

        lax.fori_loop(0, REQ_HOST, load, 0)

    part = group // 2
    width = part * TILE
    chains = [(h, c) for h in range(kv_heads) for c in range(2)]

    def flip(values, ones, target, span):
        for h in range(kv_heads):
            part = values[:, h * HD : (h + 1) * HD]
            target[h, 0:HD, span] = jnp.transpose(part).astype(jnp.bfloat16)
            target[h, HD : HD + 16, span] = ones.astype(jnp.bfloat16)

    if first:
        for copy in piece_copies:
            copy.wait()

        def flip_fresh(c, carry):
            span = pl.ds(pl.multiple_of(c * PAGE, PAGE), PAGE)
            flip(
                fresh[1, span, :].astype(jnp.float32),
                jnp.ones((16, PAGE), jnp.float32),
                fresh_flipped,
                span,
            )
            return carry

        lax.fori_loop(0, blocks // PAGE, flip_fresh, 0)

    def step(visit, row0, owned, key_of, value_of, ok, follow):
        begin = ok is not None
        rows = pl.ds(row0, TILE)
        tops = {}
        if not begin:
            for h, c in chains:
                tops[h, c] = state[visit, h, HD + 8 : HD + 9, pl.ds(c * width, width)]

        def score(h, c):
            first_head = h * group + c * part
            stacked = jnp.concatenate(
                [q[rows, pl.ds((first_head + g) * HD, HD)] for g in range(part)], axis=0
            )
            scores = lax.dot_general(
                key_of(h), stacked, (((1,), (1,)), ((), ())), preferred_element_type=jnp.float32
            )
            if begin:
                blocks_of = [scores[:, i : i + PAGE] for i in range(0, width, PAGE)]
                scores = jnp.concatenate([jnp.where(ok, x, LOW) for x in blocks_of], axis=1)
            return scores

        def mix(h, c, scores):
            lanes = pl.ds(c * width, width)
            if not begin:
                top = old_top = tops[h, c]
            if begin or follow:
                top = jnp.max(scores, axis=0, keepdims=True)
            if follow and not begin:
                top = jnp.maximum(top, old_top)
            weights = jnp.exp2((scores - top) * SCALE).astype(jnp.bfloat16)
            mixed = jnp.dot(value_of(h), weights, preferred_element_type=jnp.float32)[: HD + 8]
            if not begin:
                old = state[visit, h, 0 : HD + 8, lanes]
                if follow:
                    old = old * jnp.exp2((old_top - top) * SCALE)
                mixed = old + mixed
            state[visit, h, 0 : HD + 8, lanes] = mixed
            if begin or follow:
                state[visit, h, HD + 8 : HD + 16, lanes] = jnp.broadcast_to(top, (8, width))
            if not begin and not follow:
                peak[...] = jnp.maximum(peak[...], jnp.where(owned, mixed[HD : HD + 8], 0.0))

        scores = score(*chains[0])
        for i, chain in enumerate(chains):
            ahead = score(*chains[i + 1]) if i + 1 < len(chains) else None
            mix(*chain, scores)
            scores = ahead

    def visits_of(request):
        tiles = info[request, 3]
        return tiles if first or last else jnp.where(count[request] > 0, tiles, 0)

    def arrival(request, ready_rows):
        end_row = info[request, 2] + visits_of(request) * TILE
        need = jnp.minimum((end_row + CHUNK - 1) // CHUNK, n_chunks)

        def arrive(c, carry):
            row_copy(c).wait()
            return carry

        lax.fori_loop(ready_rows, need, arrive, 0)
        return jnp.maximum(ready_rows, need)

    def page_arrival(request):
        def page_arrive(place, carry):
            span = pl.ds(pl.multiple_of(place * PAGE, PAGE), PAGE)
            pltpu.make_async_copy(
                pages[0].at[0], kv.at[request, :, span], page_sems.at[request, place]
            ).wait()
            here = valid[request, place]
            token = lax.broadcasted_iota(jnp.int32, (PAGE, 1), 0)

            @pl.when(here < PAGE)
            def _():
                keys = kv[request, 0, span, :].astype(jnp.float32)
                kv[request, 0, span, :] = jnp.where(token < here, keys, keys[0:1, :]).astype(kv.dtype)

            values = kv[request, 1, span, :].astype(jnp.float32)
            ones = (lax.broadcasted_iota(jnp.int32, (16, PAGE), 1) < here).astype(jnp.float32)
            flip(jnp.where(token < here, values, 0.0), ones, flipped.at[request], span)
            return carry

        lax.fori_loop(0, count[request], page_arrive, 0)

    def state_out(visit):
        return pltpu.make_async_copy(state.at[visit], result.at[visit], row_sems.at[n_chunks])

    def work(request, follow):
        offset, end, begin_row, _, base = [info[request, i] for i in range(5)]
        begin_row = pl.multiple_of(begin_row, 16)
        n = count[request]

        def tile(i, carry):
            visit = base + i
            row0 = pl.multiple_of(begin_row + i * TILE, 16)
            position = row0 + lax.rem(lax.broadcasted_iota(jnp.int32, (1, width), 1), TILE)
            owned = (position >= offset) & (position < end)

            def page_step(place, pages_now):
                span = pl.ds(pl.multiple_of(place * PAGE, PAGE), pages_now * PAGE)
                step(
                    visit,
                    row0,
                    owned,
                    lambda h: kv[request, 0, span, pl.ds(h * HD, HD)],
                    lambda h: flipped[request, h, :, span],
                    None,
                    follow,
                )

            if first:
                key0 = pl.multiple_of((offset // PAGE) * PAGE, PAGE)

                def fresh_step(reach):
                    span = pl.ds(key0, reach)
                    key = key0 + lax.broadcasted_iota(jnp.int32, (reach, PAGE), 0)
                    key = jnp.where(key >= offset, key, blocks + REACH)
                    lane = lax.broadcasted_iota(jnp.int32, (reach, PAGE), 1)
                    step(
                        visit,
                        row0,
                        owned,
                        lambda h: fresh[0, span, pl.ds(h * HD, HD)],
                        lambda h: fresh_flipped[h, :, span],
                        key <= row0 + lane % TILE,
                        follow,
                    )

                near = row0 + TILE - key0 <= REACH // 2

                @pl.when(near)
                def _():
                    fresh_step(REACH // 2)

                @pl.when(jnp.logical_not(near))
                def _():
                    fresh_step(REACH)

            elif not follow:
                state_copy(visit).wait()

            def four(j, carry):
                page_step(4 * j, 4)
                return carry

            lax.fori_loop(0, n // 4, four, 0)

            @pl.when(n % 4 >= 2)
            def _():
                page_step((n // 4) * 4, 2)

            @pl.when(n % 2 == 1)
            def _():
                page_step(n - 1, 1)

            if last:
                top_rows = pl.ds(row0, 16)
                position = row0 + lax.broadcasted_iota(jnp.int32, (16, 1), 0)
                for h in range(kv_heads):
                    share = state[visit, h, 0:HD, :]
                    share = share * (1.0 / state[visit, h, HD : HD + 1, :])
                    share = jnp.transpose(share)
                    for g in range(group):
                        columns = pl.ds((h * group + g) * HD, HD)
                        rows = share[g * TILE : (g + 1) * TILE]
                        old = outs[top_rows, columns].astype(jnp.float32)
                        outs[top_rows, columns] = jnp.where(
                            position >= offset, rows[:16], old
                        ).astype(outs.dtype)
                        outs[pl.ds(row0 + 16, TILE - 16), columns] = rows[16:].astype(outs.dtype)
            return carry

        lax.fori_loop(0, visits_of(request), tile, 0)

    def out_copy(c):
        span = pl.ds(pl.multiple_of(c * CHUNK, CHUNK), CHUNK)
        return pltpu.make_async_copy(outs.at[span], result.at[span], out_sems.at[c])

    def one_request(request, ready):
        ready_rows, ready_out = ready
        ready_rows = arrival(request, ready_rows)
        page_arrival(request)
        base, tiles = info[request, 4], visits_of(request)
        peak[...] = jnp.zeros_like(peak)
        work(request, False)

        @pl.when(jnp.logical_not(jnp.max(peak[...]) <= LIMIT))
        def _():
            if not first:

                def again(i, carry):
                    state_copy(base + i).start()
                    state_copy(base + i).wait()
                    return carry

                lax.fori_loop(0, tiles, again, 0)
            work(request, True)

        if last:
            done = info[request, 1] // 16 * 16 // CHUNK

            def send(c, carry):
                out_copy(c).start()
                return carry

            lax.fori_loop(ready_out, done, send, 0)
            return (ready_rows, done)

        def store(i, carry):
            state_out(base + i).start()
            return carry

        lax.fori_loop(0, tiles, store, 0)
        return (ready_rows, ready_out)

    ready, _ = lax.fori_loop(0, REQ_HOST, one_request, (jnp.int32(0), jnp.int32(0)))

    def drain(c, carry):
        row_copy(c).wait()
        return carry

    lax.fori_loop(ready, n_chunks, drain, 0)
    if last:
        for c in range(n_chunks):
            out_copy(c).wait()
    else:

        def stored(request, carry):
            def stored_one(i, carry):
                state_out(0).wait()
                return carry

            return lax.fori_loop(0, visits_of(request), stored_one, carry)

        lax.fori_loop(0, REQ_HOST, stored, 0)


def stage(partners, stores, slots, tables, queries, pages, pieces, state, last, carried=()):
    rows, width = queries.shape
    kv_width = pages[0].shape[3]
    first = state is None
    heads, kv_heads = width // HD, kv_width // HD
    plan = dict(
        partners=partners,
        stores=stores,
        slots=slots,
        first=first,
        last=last,
        rows=rows,
        heads=heads,
        kv_heads=kv_heads,
        pieces=len(pieces),
        carried=len(carried),
    )
    visits = (rows + REQ_HOST * (15 + TILE - 1)) // TILE
    state_shape = (visits, kv_heads, HD + 16, heads // kv_heads * TILE)
    n_chunks = rows // CHUNK
    scratch = [
        pltpu.VMEM((rows + TILE, width), queries.dtype),
        pltpu.VMEM(state_shape, jnp.float32),
        pltpu.VMEM((REQ_HOST, 2, PAGES_MAX * PAGE, kv_width), queries.dtype),
        pltpu.VMEM((REQ_HOST, kv_heads, HD + 16, PAGES_MAX * PAGE), queries.dtype),
        pltpu.VMEM((8, heads // kv_heads // 2 * TILE), jnp.float32),
        pltpu.SMEM((REQ_HOST, 5), jnp.int32),
        pltpu.SMEM((REQ_HOST,), jnp.int32),
        pltpu.SMEM((REQ_HOST, PAGES_MAX), jnp.int32),
        pltpu.SMEM((stores,), jnp.int32),
        pltpu.SemaphoreType.DMA((REQ_HOST, PAGES_MAX)),
        pltpu.SemaphoreType.DMA((n_chunks + 1,)),
        pltpu.SemaphoreType.DMA((visits,)),
    ]
    if first:
        scratch += [
            pltpu.VMEM((2, rows + REACH, kv_width), queries.dtype),
            pltpu.VMEM((kv_heads, HD + 16, rows + REACH), queries.dtype),
            pltpu.SemaphoreType.DMA((len(pieces),)),
        ]
    if last:
        scratch += [
            pltpu.VMEM((rows + TILE, width), queries.dtype),
            pltpu.SemaphoreType.DMA((n_chunks,)),
        ]
    operands = list(tables) + [queries] + pages + pieces + ([] if first else [state]) + list(carried)
    n = len(operands) - len(carried)
    aliases = {} if first or last else {n - 1: 0}
    aliases |= {n + i: 1 + i for i in range(len(carried))}
    keys = len(partners) * PAGE + (MOST_NEW if first else 0)
    result, *carried = pl.pallas_call(
        functools.partial(stage_kernel, plan),
        out_shape=[
            jax.ShapeDtypeStruct(queries.shape, queries.dtype)
            if last
            else jax.ShapeDtypeStruct(state_shape, jnp.float32)
        ]
        + [jax.ShapeDtypeStruct(x.shape, x.dtype) for x in carried],
        in_specs=[SMEM] * 3 + [ANY] * (len(operands) - 3),
        out_specs=[ANY] * (1 + len(carried)),
        scratch_shapes=scratch,
        input_output_aliases=aliases,
        compiler_params=pltpu.CompilerParams(vmem_limit_bytes=VMEM_LIMIT),
        cost_estimate=pl.CostEstimate(
            flops=4 * rows * width * keys,
            bytes_accessed=rows * width * 16,
            transcendentals=rows * heads * keys,
        ),
        name="attend",
    )(*operands)
    return result, carried


def swap(values, axis, size, partner):
    return lax.ppermute(values, axis, [(i, i ^ partner) for i in range(size)])


def local(queries, fresh_kv, page_pool, page_host, page_slot, prefix_len, fresh_len):
    stores, tps = lax.axis_size("store"), lax.axis_size("tp")
    slots, head_width = page_pool.shape[0], page_pool.shape[3]
    capacity = max(2, (ENTRIES + stores - 1) // stores)

    partners = list(range(1, stores))
    far = [d for d in partners if d & (stores // 2)]
    near = [d for d in partners if not d & (stores // 2)]
    half = len(far) // 2
    early, late = far[:half], far[half:]

    in_use = jnp.arange(PAGES_MAX, dtype=jnp.int32)[None, :] * PAGE < prefix_len[:, None]
    code = jnp.where(in_use, page_host * slots + page_slot, -1)
    both = jnp.concatenate([code, swap(code, "store", stores, 1)], axis=0)
    codes = [both] + [swap(both, "store", stores, d) for d in range(2, stores, 2)]

    tp_me = lax.axis_index("tp")

    def piece(d):
        return lax.dynamic_slice_in_dim(
            fresh_kv, lax.bitwise_xor(tp_me, jnp.int32(d)) * head_width, head_width, 2
        )

    pieces = [piece(0)] + [swap(piece(d), "tp", tps, d) for d in range(1, tps)]
    sent = collect(early, capacity, codes, page_pool, pieces)
    arrived = {d: swap(pages, "store", stores, d) for d, pages in zip(early, sent)}

    def attend(partners, pages, pieces, state, last, carried):
        tables = (code, prefix_len, fresh_len)
        return stage(
            partners, stores, slots, tables, queries, pages, pieces, state, last, carried
        )

    state, codes = attend([0], [page_pool], pieces, None, False, codes)
    *sent, waiting = collect(near + late, capacity, codes, page_pool, [])
    arrived |= {d: swap(pages, "store", stores, d) for d, pages in zip(near + late, sent)}
    state, (waiting,) = attend(early, [arrived[d] for d in early], [], state, False, [waiting])
    arrived[late[-1]] = swap(waiting, "store", stores, late[-1])
    for part in (near, late[:-1], late[-1:]):
        state, _ = attend(part, [arrived[d] for d in part], [], state, part == late[-1:], [])
    return state


def solution(mesh):
    placed = (
        P("store", "tp"),
        P(None, ("store", "tp"), None),
        P("store", None, None, "tp"),
        P("store", None),
        P("store", None),
        P("store"),
        P("store", None),
    )
    return jax.shard_map(
        local, mesh=mesh, in_specs=placed, out_specs=P("store", "tp"), check_vma=False
    )
```

```python
import functools
import math

import jax
import jax.numpy as jnp
from jax import lax
from jax.experimental import pallas as pl
from jax.experimental.pallas import tpu as pltpu
from jax.sharding import PartitionSpec as P

HD = 128
REQ_HOST = 4
PAGE = 128
PAGES_MAX = 8
MOST_NEW = 384
ENTRIES = REQ_HOST * PAGES_MAX

TILE = 64
REACH = 512
CHUNK = 256
OUT_CHUNK = 128
SCALE = math.log2(math.e) / math.sqrt(HD)
LOW = -3e38
LIMIT = 2.0**60

ANY = pl.BlockSpec(memory_space=pl.ANY)
SMEM = pl.BlockSpec(memory_space=pltpu.SMEM)
VMEM = pl.BlockSpec(memory_space=pltpu.VMEM)
SMALL = pl.CostEstimate(flops=0, bytes_accessed=2**16, transcendentals=0)
VMEM_LIMIT = 24 * 2**20


def in_hbm(values):
    return pltpu.with_memory_space_constraint(values, pltpu.HBM)


def gather(parcels, slots, codes, pool, sends, chosen, sems):
    me = lax.axis_index("store")

    def take(i, rank, slot):
        return pltpu.make_async_copy(pool.at[slot], sends[i].at[rank], sems.at[i, rank])

    for i, (partner, ranks) in enumerate(parcels):
        for rank in range(ranks[-1] + 1):
            chosen[rank] = 0
        table, first_row = codes[partner // 2], REQ_HOST * (partner % 2)

        def scan(entry, found, table=table, first_row=first_row):
            code = table[first_row + entry // PAGES_MAX, entry % PAGES_MAX] - me * slots
            hit = (code >= 0) & (code < slots)
            chosen[found] = jnp.where(hit, code, 0)
            return found + hit.astype(jnp.int32)

        lax.fori_loop(0, ENTRIES, scan, jnp.int32(0), unroll=8)
        for rank in ranks:
            take(i, rank - ranks[0], chosen[rank]).start()

    def wait():
        for i, (_, ranks) in enumerate(parcels):
            for rank in range(len(ranks)):
                take(i, rank, 0).wait()

    return wait


def gather_shapes(parcels, pool):
    return [pltpu.VMEM((len(ranks),) + pool.shape[1:], pool.dtype) for _, ranks in parcels]


def gather_scratch(parcels):
    most = max(ranks[-1] + 1 for _, ranks in parcels)
    return [pltpu.SMEM((most + 2,), jnp.int32), pltpu.SemaphoreType.DMA((len(parcels), most))]


def pairs_of(parcels):
    return sorted({partner // 2 for partner, _ in parcels})


def collect_kernel(parcels, slots, *refs):
    refs = list(refs)
    take_refs = lambda count: [refs.pop(0) for _ in range(count)]
    pairs = pairs_of(parcels)
    codes, (pool,) = dict(zip(pairs, take_refs(len(pairs)))), take_refs(1)
    gather(parcels, slots, codes, pool, take_refs(len(parcels)), *refs)()


def collect(parcels, codes, pool):
    codes = [codes[i] for i in pairs_of(parcels)]
    return pl.pallas_call(
        functools.partial(collect_kernel, parcels, pool.shape[0]),
        out_shape=gather_shapes(parcels, pool),
        in_specs=[SMEM] * len(codes) + [ANY],
        out_specs=[ANY] * len(parcels),
        scratch_shapes=gather_scratch(parcels),
        compiler_params=pltpu.CompilerParams(vmem_limit_bytes=VMEM_LIMIT),
        cost_estimate=SMALL,
        name="collect",
    )(*codes, in_hbm(pool))


def stage_kernel(plan, *refs):
    parcels, first, finish, last = plan["parcels"], plan["first"], plan["finish"], plan["last"]
    blocks, heads, kv_heads = plan["rows"], plan["heads"], plan["kv_heads"]
    group = heads // kv_heads
    refs = list(refs)
    take = lambda n: [refs.pop(0) for _ in range(n)]
    codes, prefix, lengths = take(3)
    if first:
        all_codes = dict(zip(plan["pairs"], take(len(plan["pairs"]))))
        (queries,) = take(1)
    pages = take(len(parcels))
    pieces = take(plan["pieces"]) if first else []
    if not first:
        take(3 if last else 2)
    take(plan["carried"])
    state, q = take(2)
    if finish or last:
        (outs,) = take(1)
    if last:
        (result,) = take(1)
    take(plan["carried"])
    sends = take(len(plan["others"]))
    kv, flipped, peak, info, count, later, valid, counters, page_sems, row_sems = take(10)
    if first:
        fresh, fresh_flipped, fresh_sems = take(3)
        chosen, send_sems = take(2)
    else:
        (backup,) = take(1)
    if last:
        (out_sems,) = take(1)
    me = lax.axis_index("store")
    n_chunks = blocks // CHUNK

    def row_copy(c):
        span = pl.ds(pl.multiple_of(c * CHUNK, CHUNK), CHUNK)
        return pltpu.make_async_copy(queries.at[span], q.at[span], row_sems.at[c])

    offset, base = jnp.int32(0), jnp.int32(0)
    for request in range(REQ_HOST):
        end = offset + lengths[0, request]
        begin_row = (offset // 16) * 16
        tiles = (end - begin_row + TILE - 1) // TILE
        for i, value in enumerate((offset, end, begin_row, tiles, base)):
            info[request, i] = value
        offset, base = end, base + tiles
        count[request] = 0
        later[request] = 0
    for owner in range(plan["stores"]):
        counters[owner] = 0

    def fetch(entry, carry):
        request, page = entry // PAGES_MAX, entry % PAGES_MAX
        code = codes[request, page]
        used = code >= 0
        code = jnp.maximum(code, 0)
        owner, slot = lax.div(code, plan["slots"]), lax.rem(code, plan["slots"])
        rank = counters[owner]
        counters[owner] = rank + used.astype(jnp.int32)
        place = count[request]
        here = jnp.bool_(False)

        def within(parcel):
            partner, ranks = parcel
            mine = used & (owner == lax.bitwise_xor(me, jnp.int32(partner)))
            return mine & (rank >= ranks[0]) & (rank <= ranks[-1])

        for parcel in plan["rest"]:
            later[request] = later[request] | within(parcel).astype(jnp.int32)
        for i, (partner, ranks) in enumerate(parcels):
            mine = within((partner, ranks))
            index = slot if partner == 0 else rank - ranks[0]

            @pl.when(mine)
            def _(i=i, index=index):
                span = pl.ds(pl.multiple_of(place * PAGE, PAGE), PAGE)
                pltpu.make_async_copy(
                    pages[i].at[index], kv.at[request, :, span], page_sems.at[request, place]
                ).start()

            here = here | mine

        @pl.when(here)
        def _():
            valid[request, place] = jnp.minimum(prefix[request] - page * PAGE, PAGE)
            count[request] = place + 1

        return carry

    if first:
        tp_me = lax.axis_index("tp")
        piece_copies = []
        for i in range(len(pieces)):
            n = pieces[i].shape[1]
            span = pl.ds(pl.multiple_of(lax.bitwise_xor(tp_me, jnp.int32(i)) * n, n), n)
            piece_copies.append(pltpu.make_async_copy(pieces[i], fresh.at[:, span], fresh_sems.at[i]))
            piece_copies[-1].start()
        rest = pl.ds(blocks, REACH)
        fresh[0, rest, :] = jnp.zeros((REACH, fresh.shape[2]), fresh.dtype)
        fresh_flipped[:, :, rest] = jnp.zeros((kv_heads, HD + 16, REACH), fresh.dtype)
    if first:
        for c in range(n_chunks):
            row_copy(c).start()
    lax.fori_loop(0, ENTRIES, fetch, 0)
    if first:
        wait_sends = gather(
            plan["others"], plan["slots"], all_codes, pages[0], sends, chosen, send_sems
        )

    part = group // 2
    width = part * TILE
    chains = [(h, c) for h in range(kv_heads) for c in range(2)]

    def flip(values, ones, target, span):
        for h in range(kv_heads):
            part = values[:, h * HD : (h + 1) * HD]
            target[h, 0:HD, span] = jnp.transpose(part).astype(jnp.bfloat16)
            target[h, HD : HD + 16, span] = ones.astype(jnp.bfloat16)

    if first:
        for copy in piece_copies:
            copy.wait()

        def flip_fresh(c, carry):
            span = pl.ds(pl.multiple_of(c * PAGE, PAGE), PAGE)
            flip(
                fresh[1, span, :].astype(jnp.float32),
                jnp.ones((16, PAGE), jnp.float32),
                fresh_flipped,
                span,
            )
            return carry

        lax.fori_loop(0, blocks // PAGE, flip_fresh, 0)

    def step(visit, row0, owned, key_of, value_of, ok, follow):
        begin = ok is not None
        rows = pl.ds(row0, TILE)
        tops = {}
        if not begin:
            for h, c in chains:
                tops[h, c] = state[visit, h, HD + 8 : HD + 9, pl.ds(c * width, width)]

        def score(h, c):
            first_head = h * group + c * part
            stacked = jnp.concatenate(
                [q[rows, pl.ds((first_head + g) * HD, HD)] for g in range(part)], axis=0
            )
            scores = lax.dot_general(
                key_of(h), stacked, (((1,), (1,)), ((), ())), preferred_element_type=jnp.float32
            )
            if begin:
                blocks_of = [scores[:, i : i + PAGE] for i in range(0, width, PAGE)]
                scores = jnp.concatenate([jnp.where(ok, x, LOW) for x in blocks_of], axis=1)
            return scores

        def reference(h, c, scores):
            if begin:
                return jnp.max(scores, axis=0, keepdims=True)
            if follow:
                return jnp.maximum(jnp.max(scores, axis=0, keepdims=True), tops[h, c])
            return tops[h, c]

        def update(h, c, top, mixed):
            lanes = pl.ds(c * width, width)
            if not begin:
                old = state[visit, h, 0 : HD + 8, lanes]
                if follow:
                    old = old * jnp.exp2((tops[h, c] - top) * SCALE)
                mixed = old + mixed
            state[visit, h, 0 : HD + 8, lanes] = mixed
            if begin or follow:
                state[visit, h, HD + 8 : HD + 16, lanes] = jnp.broadcast_to(top, (8, width))
            if not begin and not follow:
                peak[...] = jnp.maximum(peak[...], jnp.where(owned, mixed[HD : HD + 8], 0.0))

        scores = [score(h, c) for h, c in chains]
        new_tops = [reference(h, c, x) for (h, c), x in zip(chains, scores)]
        weights = [
            jnp.exp2((x - top) * SCALE).astype(jnp.bfloat16) for x, top in zip(scores, new_tops)
        ]
        mixed = [
            jnp.dot(value_of(h), x, preferred_element_type=jnp.float32)[: HD + 8]
            for (h, c), x in zip(chains, weights)
        ]
        for (h, c), top, x in zip(chains, new_tops, mixed):
            update(h, c, top, x)

    def visits_of(request):
        tiles = info[request, 3]
        return tiles if first or finish else jnp.where(count[request] > 0, tiles, 0)

    def arrival(request, ready_rows):
        end_row = info[request, 2] + visits_of(request) * TILE
        need = jnp.minimum((end_row + CHUNK - 1) // CHUNK, n_chunks)

        def arrive(c, carry):
            row_copy(c).wait()
            return carry

        lax.fori_loop(ready_rows, need, arrive, 0)
        return jnp.maximum(ready_rows, need)

    def page_arrival(request):
        def page_arrive(place, carry):
            span = pl.ds(pl.multiple_of(place * PAGE, PAGE), PAGE)
            pltpu.make_async_copy(
                pages[0].at[0], kv.at[request, :, span], page_sems.at[request, place]
            ).wait()
            here = valid[request, place]
            token = lax.broadcasted_iota(jnp.int32, (PAGE, 1), 0)

            @pl.when(here < PAGE)
            def _():
                keys = kv[request, 0, span, :].astype(jnp.float32)
                kv[request, 0, span, :] = jnp.where(token < here, keys, keys[0:1, :]).astype(kv.dtype)

            values = kv[request, 1, span, :].astype(jnp.float32)
            ones = (lax.broadcasted_iota(jnp.int32, (16, PAGE), 1) < here).astype(jnp.float32)
            flip(jnp.where(token < here, values, 0.0), ones, flipped.at[request], span)
            return carry

        lax.fori_loop(0, count[request], page_arrive, 0)

    def work(request, follow):
        offset, end, begin_row, _, base = [info[request, i] for i in range(5)]
        begin_row = pl.multiple_of(begin_row, 16)
        n = count[request]

        def tile(i, carry):
            visit = base + i
            row0 = pl.multiple_of(begin_row + i * TILE, 16)
            position = row0 + lax.rem(lax.broadcasted_iota(jnp.int32, (1, width), 1), TILE)
            owned = (position >= offset) & (position < end)

            def page_step(place, pages_now):
                span = pl.ds(pl.multiple_of(place * PAGE, PAGE), pages_now * PAGE)
                step(
                    visit,
                    row0,
                    owned,
                    lambda h: kv[request, 0, span, pl.ds(h * HD, HD)],
                    lambda h: flipped[request, h, :, span],
                    None,
                    follow,
                )

            if first:
                key0 = pl.multiple_of((offset // PAGE) * PAGE, PAGE)

                def fresh_step(reach):
                    span = pl.ds(key0, reach)
                    key = key0 + lax.broadcasted_iota(jnp.int32, (reach, PAGE), 0)
                    key = jnp.where(key >= offset, key, blocks + REACH)
                    lane = lax.broadcasted_iota(jnp.int32, (reach, PAGE), 1)
                    step(
                        visit,
                        row0,
                        owned,
                        lambda h: fresh[0, span, pl.ds(h * HD, HD)],
                        lambda h: fresh_flipped[h, :, span],
                        key <= row0 + lane % TILE,
                        follow,
                    )

                near = row0 + TILE - key0 <= REACH // 2

                @pl.when(near)
                def _():
                    fresh_step(REACH // 2)

                @pl.when(jnp.logical_not(near))
                def _():
                    fresh_step(REACH)

            else:
                if follow:
                    state[visit] = backup[i]
                else:
                    backup[i] = state[visit]

            def four(j, carry):
                page_step(4 * j, 4)
                return carry

            lax.fori_loop(0, n // 4, four, 0)

            for rest in (1, 2, 3):

                @pl.when(n % 4 == rest)
                def _(rest=rest):
                    page_step((n // 4) * 4, rest)

            if finish or last:
                def put(kept):
                    position = row0 + lax.broadcasted_iota(jnp.int32, (kept, 1), 0)
                    mine = (position >= offset) & (position < end)
                    for h in range(kv_heads):
                        share = state[visit, h, 0:HD, :]
                        share = share * (1.0 / state[visit, h, HD : HD + 1, :])
                        share = jnp.transpose(share.astype(outs.dtype))
                        for g in range(group):
                            columns = pl.ds((h * group + g) * HD, HD)
                            rows = share[g * TILE : (g + 1) * TILE]
                            old = outs[pl.ds(row0, kept), columns].astype(jnp.float32)
                            new = jnp.where(mine, rows[:kept].astype(jnp.float32), old)
                            outs[pl.ds(row0, kept), columns] = new.astype(outs.dtype)
                            if kept < TILE:
                                outs[pl.ds(row0 + kept, TILE - kept), columns] = rows[kept:]

                if finish:

                    @pl.when(later[request] == 0)
                    def _():
                        put(16)

                else:

                    @pl.when(row0 + TILE <= end)
                    def _():
                        put(16)

                    @pl.when(row0 + TILE > end)
                    def _():
                        put(TILE)

            return carry

        lax.fori_loop(0, visits_of(request), tile, 0)

    def out_copy(c):
        span = pl.ds(pl.multiple_of(c * OUT_CHUNK, OUT_CHUNK), OUT_CHUNK)
        return pltpu.make_async_copy(outs.at[span], result.at[span], out_sems.at[c])

    def out_ready(c):
        ready = jnp.bool_(True)
        for request in range(REQ_HOST):
            apart = (info[request, 1] <= c * OUT_CHUNK) | (info[request, 0] >= (c + 1) * OUT_CHUNK)
            ready = ready & (apart | (count[request] == 0))
        return ready

    def send_out(wanted):
        for c in range(blocks // OUT_CHUNK):

            @pl.when(out_ready(c) == wanted)
            def _(c=c):
                out_copy(c).start()

    def one_request(request, ready_rows):
        if first:
            ready_rows = arrival(request, ready_rows)
        page_arrival(request)
        peak[...] = jnp.zeros_like(peak)
        work(request, False)

        @pl.when(jnp.logical_not(jnp.max(peak[...]) <= LIMIT))
        def _():
            work(request, True)

        return ready_rows

    if last:
        send_out(True)
    lax.fori_loop(0, REQ_HOST, one_request, jnp.int32(0))
    if first:
        wait_sends()
    if last:
        send_out(False)
        for c in range(blocks // OUT_CHUNK):
            out_copy(c).wait()


def stage(
    parcels, rest, stores, slots, tables, queries, pages, start, held, finish, last, carried
):
    pieces, codes, others = start
    rows, width = queries.shape
    kv_width = pages[0].shape[3]
    first = held is None
    heads, kv_heads = width // HD, kv_width // HD
    plan = dict(
        parcels=parcels,
        rest=rest,
        stores=stores,
        slots=slots,
        first=first,
        finish=finish,
        last=last,
        rows=rows,
        heads=heads,
        kv_heads=kv_heads,
        pieces=len(pieces),
        carried=len(carried),
        pairs=pairs_of(others),
        others=others,
    )
    visits = (rows + REQ_HOST * (15 + TILE - 1)) // TILE
    most = (MOST_NEW + 15 + TILE - 1) // TILE
    visit_shape = (kv_heads, HD + 16, heads // kv_heads * TILE)
    n_chunks = rows // CHUNK
    scratch = [
        pltpu.VMEM((REQ_HOST, 2, PAGES_MAX * PAGE, kv_width), queries.dtype),
        pltpu.VMEM((REQ_HOST, kv_heads, HD + 16, PAGES_MAX * PAGE), queries.dtype),
        pltpu.VMEM((8, heads // kv_heads // 2 * TILE), jnp.float32),
        pltpu.SMEM((REQ_HOST, 5), jnp.int32),
        pltpu.SMEM((REQ_HOST,), jnp.int32),
        pltpu.SMEM((REQ_HOST,), jnp.int32),
        pltpu.SMEM((REQ_HOST, PAGES_MAX), jnp.int32),
        pltpu.SMEM((stores,), jnp.int32),
        pltpu.SemaphoreType.DMA((REQ_HOST, PAGES_MAX)),
        pltpu.SemaphoreType.DMA((n_chunks,)),
    ]
    if first:
        scratch += [
            pltpu.VMEM((2, rows + REACH, kv_width), queries.dtype),
            pltpu.VMEM((kv_heads, HD + 16, rows + REACH), queries.dtype),
            pltpu.SemaphoreType.DMA((len(pieces),)),
        ] + gather_scratch(others)
    else:
        scratch += [pltpu.VMEM((most,) + visit_shape, jnp.float32)]
    if last:
        scratch += [pltpu.SemaphoreType.DMA((rows // OUT_CHUNK,))]
    operands = list(tables) + [codes[i] for i in pairs_of(others)]
    specs = [SMEM] * len(operands)
    operands += ([in_hbm(queries)] if first else []) + pages + pieces
    specs += [ANY] * (len(operands) - len(specs))
    wide = pltpu.VMEM((rows + TILE, width), queries.dtype)
    out_shape = [pltpu.VMEM((visits,) + visit_shape, jnp.float32), wide]
    if finish or last:
        out_shape += [wide]
    n_held = len(out_shape)
    aliases = {}
    if not first:
        aliases = {len(operands) + i: i for i in range(len(held))}
        operands += list(held)
        specs += [VMEM] * len(held)
    if last:
        out_shape += [jax.ShapeDtypeStruct(queries.shape, queries.dtype)]
    aliases |= {len(operands) + i: len(out_shape) + i for i in range(len(carried))}
    out_specs = [VMEM] * n_held + [ANY] * (last + len(carried) + len(others))
    out_shape += [jax.ShapeDtypeStruct(x.shape, x.dtype) for x in carried]
    out_shape += gather_shapes(others, pages[0])
    results = pl.pallas_call(
        functools.partial(stage_kernel, plan),
        out_shape=out_shape,
        in_specs=specs + [ANY] * len(carried),
        out_specs=out_specs,
        scratch_shapes=scratch,
        input_output_aliases=aliases,
        compiler_params=pltpu.CompilerParams(vmem_limit_bytes=VMEM_LIMIT),
        cost_estimate=SMALL,
        name="attend",
    )(*operands, *carried)
    return results[:n_held], results[n_held : n_held + last], results[n_held + last :]


def swap(values, axis, size, partner):
    return lax.ppermute(values, axis, [(i, i ^ partner) for i in range(size)])


def local(queries, fresh_kv, page_pool, page_host, page_slot, prefix_len, fresh_len):
    stores, tps = lax.axis_size("store"), lax.axis_size("tp")
    slots, head_width = page_pool.shape[0], page_pool.shape[3]
    capacity = max(2, (ENTRIES + stores - 1) // stores)

    partners = list(range(1, stores))
    far = [d for d in partners if d & (stores // 2)]
    near = [d for d in partners if not d & (stores // 2)]
    half = len(far) // 2
    every = tuple(range(capacity))
    near = [(d, every) for d in near]
    early, late = [[(d, every) for d in part] for part in (far[:half], far[half:])]
    cut = max(1, capacity * 3 // 4)
    late, final = [[(d, ranks) for d, _ in late] for ranks in (every[:cut], every[cut:])]

    in_use = jnp.arange(PAGES_MAX, dtype=jnp.int32)[None, :] * PAGE < prefix_len[:, None]
    code = jnp.where(in_use, page_host * slots + page_slot, -1)
    both = jnp.concatenate([code, swap(code, "store", stores, 1)], axis=0)
    codes = [both] + [swap(both, "store", stores, d) for d in range(2, stores, 2)]

    tp_me = lax.axis_index("tp")

    def piece(d):
        return lax.dynamic_slice_in_dim(
            fresh_kv, lax.bitwise_xor(tp_me, jnp.int32(d)) * head_width, head_width, 2
        )

    pieces = [piece(0)] + [swap(piece(d), "tp", tps, d) for d in range(1, tps)]
    def send(parcels, pages):
        return {p: swap(x, "store", stores, p[0]) for p, x in zip(parcels, pages)}

    arrived = send(early + near, collect(early + near, codes, page_pool))

    def attend(parcels, held, carried=(), start=([], [], []), finish=False, last=False):
        pages = [arrived[p] for p in parcels] if held else [in_hbm(page_pool)]
        return stage(
            parcels,
            final if finish else [],
            stores,
            slots,
            (code, prefix_len, fresh_len),
            queries,
            pages,
            start,
            held,
            finish,
            last,
            carried,
        )

    local_pages = [(0, tuple(range(ENTRIES)))]
    held, _, others = attend(local_pages, None, start=(pieces, codes, late + final))
    arrived |= send(late, others[: len(late)])
    held, _, others = attend(near, held, others[len(late) :])
    held, _, others = attend(early, held, others)
    arrived |= send(final, others)
    held, _, _ = attend(late, held, finish=True)
    _, (out,), _ = attend(final, held, last=True)
    return out


def solution(mesh):
    placed = (
        P("store", "tp"),
        P(None, ("store", "tp"), None),
        P("store", None, None, "tp"),
        P("store", None),
        P("store", None),
        P("store"),
        P("store", None),
    )
    return jax.shard_map(
        local, mesh=mesh, in_specs=placed, out_specs=P("store", "tp"), check_vma=False
    )
```

```python
import functools
import math

import jax
import jax.numpy as jnp
from jax import lax
from jax.experimental import pallas as pl
from jax.experimental.pallas import tpu as pltpu
from jax.sharding import PartitionSpec as P

HD = 128
REQ_HOST = 4
PAGE = 128
PAGES_MAX = 8
MOST_NEW = 384
ENTRIES = REQ_HOST * PAGES_MAX

TILE = 64
REACH = 512
CHUNK = 256
OUT_CHUNK = 128
SCALE = math.log2(math.e) / math.sqrt(HD)
LOW = -3e38
LIMIT = 2.0**60

ANY = pl.BlockSpec(memory_space=pl.ANY)
SMEM = pl.BlockSpec(memory_space=pltpu.SMEM)
VMEM = pl.BlockSpec(memory_space=pltpu.VMEM)
SMALL = pl.CostEstimate(flops=0, bytes_accessed=2**16, transcendentals=0)
VMEM_LIMIT = 24 * 2**20


def in_hbm(values):
    return pltpu.with_memory_space_constraint(values, pltpu.HBM)


def gather(parcels, slots, codes, pool, sends, chosen, sems):
    me = lax.axis_index("store")

    def take(i, rank, slot):
        return pltpu.make_async_copy(pool.at[slot], sends[i].at[rank], sems.at[i, rank])

    for i, (partner, ranks) in enumerate(parcels):
        for rank in range(ranks[-1] + 1):
            chosen[rank] = 0
        table, first_row = codes[partner // 2], REQ_HOST * (partner % 2)

        def scan(entry, found, table=table, first_row=first_row):
            code = table[first_row + entry // PAGES_MAX, entry % PAGES_MAX] - me * slots
            hit = (code >= 0) & (code < slots)
            chosen[found] = jnp.where(hit, code, 0)
            return found + hit.astype(jnp.int32)

        lax.fori_loop(0, ENTRIES, scan, jnp.int32(0), unroll=8)
        for rank in ranks:
            take(i, rank - ranks[0], chosen[rank]).start()

    def wait():
        for i, (_, ranks) in enumerate(parcels):
            for rank in range(len(ranks)):
                take(i, rank, 0).wait()

    return wait


def gather_shapes(parcels, pool):
    return [pltpu.VMEM((len(ranks),) + pool.shape[1:], pool.dtype) for _, ranks in parcels]


def gather_scratch(parcels):
    most = max(ranks[-1] + 1 for _, ranks in parcels)
    return [pltpu.SMEM((most + 2,), jnp.int32), pltpu.SemaphoreType.DMA((len(parcels), most))]


def pairs_of(parcels):
    return sorted({partner // 2 for partner, _ in parcels})


def collect_kernel(parcels, slots, *refs):
    refs = list(refs)
    take_refs = lambda count: [refs.pop(0) for _ in range(count)]
    pairs = pairs_of(parcels)
    codes, (pool,) = dict(zip(pairs, take_refs(len(pairs)))), take_refs(1)
    gather(parcels, slots, codes, pool, take_refs(len(parcels)), *refs)()


def collect(parcels, codes, pool):
    codes = [codes[i] for i in pairs_of(parcels)]
    return pl.pallas_call(
        functools.partial(collect_kernel, parcels, pool.shape[0]),
        out_shape=gather_shapes(parcels, pool),
        in_specs=[SMEM] * len(codes) + [ANY],
        out_specs=[ANY] * len(parcels),
        scratch_shapes=gather_scratch(parcels),
        compiler_params=pltpu.CompilerParams(vmem_limit_bytes=VMEM_LIMIT),
        cost_estimate=SMALL,
        name="collect",
    )(*codes, in_hbm(pool))


def stage_kernel(plan, *refs):
    parcels, first, finish, last = plan["parcels"], plan["first"], plan["finish"], plan["last"]
    blocks, heads, kv_heads = plan["rows"], plan["heads"], plan["kv_heads"]
    group = heads // kv_heads
    refs = list(refs)
    take = lambda n: [refs.pop(0) for _ in range(n)]
    codes, prefix, lengths = take(3)
    if first:
        all_codes = dict(zip(plan["pairs"], take(len(plan["pairs"]))))
        (queries,) = take(1)
    pages = take(len(parcels))
    pieces = take(plan["pieces"]) if first else []
    if not first:
        take(4 if last else 2)
    take(plan["carried"])
    state, q = take(2)
    if finish or last:
        (outs,) = take(1)
    if finish or last:
        (result,) = take(1)
    take(plan["carried"])
    sends = take(len(plan["others"]))
    kv, flipped, peak, info, count, later, valid, counters, page_sems, row_sems = take(10)
    if first:
        fresh, fresh_flipped, fresh_sems = take(3)
        chosen, send_sems = take(2)
    else:
        (backup,) = take(1)
    if finish or last:
        (out_sems,) = take(1)
    me = lax.axis_index("store")
    n_chunks = blocks // CHUNK

    def row_copy(c):
        span = pl.ds(pl.multiple_of(c * CHUNK, CHUNK), CHUNK)
        return pltpu.make_async_copy(queries.at[span], q.at[span], row_sems.at[c])

    offset, base = jnp.int32(0), jnp.int32(0)
    for request in range(REQ_HOST):
        end = offset + lengths[0, request]
        begin_row = (offset // 16) * 16
        tiles = (end - begin_row + TILE - 1) // TILE
        for i, value in enumerate((offset, end, begin_row, tiles, base)):
            info[request, i] = value
        offset, base = end, base + tiles
        count[request] = 0
        later[request] = 0
    for owner in range(plan["stores"]):
        counters[owner] = 0

    def fetch(entry, carry):
        request, page = entry // PAGES_MAX, entry % PAGES_MAX
        code = codes[request, page]
        used = code >= 0
        code = jnp.maximum(code, 0)
        owner, slot = lax.div(code, plan["slots"]), lax.rem(code, plan["slots"])
        rank = counters[owner]
        counters[owner] = rank + used.astype(jnp.int32)
        place = count[request]
        def within(parcel):
            partner, ranks = parcel
            mine = used & (owner == lax.bitwise_xor(me, jnp.int32(partner)))
            return mine & (rank >= ranks[0]) & (rank <= ranks[-1])

        for parcel in plan["rest"]:
            later[request] = later[request] | within(parcel).astype(jnp.int32)
        mine = [within(parcel) for parcel in parcels]

        @pl.when(functools.reduce(jnp.logical_or, mine))
        def _():
            span = pl.ds(pl.multiple_of(place * PAGE, PAGE), PAGE)
            for i, (partner, ranks) in enumerate(parcels):
                index = slot if partner == 0 else rank - ranks[0]

                @pl.when(mine[i])
                def _(i=i, index=index):
                    pltpu.make_async_copy(
                        pages[i].at[index], kv.at[request, :, span], page_sems.at[request, place]
                    ).start()

            valid[request, place] = jnp.minimum(prefix[request] - page * PAGE, PAGE)
            count[request] = place + 1

        return carry

    if first:
        tp_me = lax.axis_index("tp")
        piece_copies = []
        for i in range(len(pieces)):
            n = pieces[i].shape[1]
            span = pl.ds(pl.multiple_of(lax.bitwise_xor(tp_me, jnp.int32(i)) * n, n), n)
            piece_copies.append(pltpu.make_async_copy(pieces[i], fresh.at[:, span], fresh_sems.at[i]))
            piece_copies[-1].start()
        rest = pl.ds(blocks, REACH)
        fresh[0, rest, :] = jnp.zeros((REACH, fresh.shape[2]), fresh.dtype)
        fresh_flipped[:, :, rest] = jnp.zeros((kv_heads, HD + 16, REACH), fresh.dtype)
    if first:
        for c in range(n_chunks):
            row_copy(c).start()
    lax.fori_loop(0, ENTRIES, fetch, 0, unroll=2)
    if first:
        wait_sends = gather(
            plan["others"], plan["slots"], all_codes, pages[0], sends, chosen, send_sems
        )

    part = group // 2
    width = part * TILE
    chains = [(h, c) for h in range(kv_heads) for c in range(2)]

    def flip(values, ones, target, span):
        for h in range(kv_heads):
            part = values[:, h * HD : (h + 1) * HD]
            target[h, 0:HD, span] = jnp.transpose(part.astype(jnp.bfloat16))
            target[h, HD : HD + 16, span] = ones.astype(jnp.bfloat16)

    if first:
        for copy in piece_copies:
            copy.wait()

        def flip_fresh(c, carry):
            span = pl.ds(pl.multiple_of(c * PAGE, PAGE), PAGE)
            flip(
                fresh[1, span, :].astype(jnp.float32),
                jnp.ones((16, PAGE), jnp.float32),
                fresh_flipped,
                span,
            )
            return carry

        lax.fori_loop(0, blocks // PAGE, flip_fresh, 0)

    def step(visits, key_of, value_of, ok, follow):
        begin = ok is not None
        links = [(v, h, c) for v in range(len(visits)) for h, c in chains]
        tops = {}
        if not begin:
            for v, h, c in links:
                tops[v, h, c] = state[visits[v][0], h, HD + 8 : HD + 9, pl.ds(c * width, width)]

        def score(v, h, c):
            rows = pl.ds(visits[v][1], TILE)
            first_head = h * group + c * part
            stacked = jnp.concatenate(
                [q[rows, pl.ds((first_head + g) * HD, HD)] for g in range(part)], axis=0
            )
            scores = lax.dot_general(
                key_of(h), stacked, (((1,), (1,)), ((), ())), preferred_element_type=jnp.float32
            )
            if begin:
                blocks_of = [scores[:, i : i + PAGE] for i in range(0, width, PAGE)]
                scores = jnp.concatenate([jnp.where(ok, x, LOW) for x in blocks_of], axis=1)
            return scores

        def reference(link, scores):
            if begin:
                return jnp.max(scores, axis=0, keepdims=True)
            if follow:
                return jnp.maximum(jnp.max(scores, axis=0, keepdims=True), tops[link])
            return tops[link]

        def update(v, h, c, top, mixed):
            visit, _, owned = visits[v]
            lanes = pl.ds(c * width, width)
            if not begin:
                old = state[visit, h, 0 : HD + 8, lanes]
                if follow:
                    old = old * jnp.exp2((tops[v, h, c] - top) * SCALE)
                mixed = old + mixed
            state[visit, h, 0 : HD + 8, lanes] = mixed
            if begin or follow:
                state[visit, h, HD + 8 : HD + 16, lanes] = jnp.broadcast_to(top, (8, width))
            if not begin and not follow:
                peak[...] = jnp.maximum(peak[...], jnp.where(owned, mixed[HD : HD + 8], 0.0))

        scores = [score(*link) for link in links]
        new_tops = [reference(link, x) for link, x in zip(links, scores)]
        weights = [
            jnp.exp2((x - top) * SCALE).astype(jnp.bfloat16) for x, top in zip(scores, new_tops)
        ]
        mixed = [
            jnp.dot(value_of(link[1]), x, preferred_element_type=jnp.float32)[: HD + 8]
            for link, x in zip(links, weights)
        ]
        for link, top, x in zip(links, new_tops, mixed):
            update(*link, top, x)

    def visits_of(request):
        tiles = info[request, 3]
        return tiles if first or finish else jnp.where(count[request] > 0, tiles, 0)

    def arrival(request, ready_rows):
        end_row = info[request, 2] + visits_of(request) * TILE
        need = jnp.minimum((end_row + CHUNK - 1) // CHUNK, n_chunks)

        def arrive(c, carry):
            row_copy(c).wait()
            return carry

        lax.fori_loop(ready_rows, need, arrive, 0)
        return jnp.maximum(ready_rows, need)

    def page_arrival(request):
        def page_arrive(place, carry):
            span = pl.ds(pl.multiple_of(place * PAGE, PAGE), PAGE)
            pltpu.make_async_copy(
                pages[0].at[0], kv.at[request, :, span], page_sems.at[request, place]
            ).wait()
            here = valid[request, place]
            token = lax.broadcasted_iota(jnp.int32, (PAGE, 1), 0)

            @pl.when(here < PAGE)
            def _():
                keys = kv[request, 0, span, :].astype(jnp.float32)
                kv[request, 0, span, :] = jnp.where(token < here, keys, keys[0:1, :]).astype(kv.dtype)

            values = kv[request, 1, span, :].astype(jnp.float32)
            ones = (lax.broadcasted_iota(jnp.int32, (16, PAGE), 1) < here).astype(jnp.float32)
            flip(jnp.where(token < here, values, 0.0), ones, flipped.at[request], span)
            return carry

        lax.fori_loop(0, count[request], page_arrive, 0)

    def work(request, follow):
        offset, end, begin_row, _, base = [info[request, i] for i in range(5)]
        begin_row = pl.multiple_of(begin_row, 16)
        n = count[request]

        def one_visit(i):
            row0 = pl.multiple_of(begin_row + i * TILE, 16)
            position = row0 + lax.rem(lax.broadcasted_iota(jnp.int32, (1, width), 1), TILE)
            return (base + i, row0, (position >= offset) & (position < end))

        def page_step(visits, place, pages_now):
            span = pl.ds(pl.multiple_of(place * PAGE, PAGE), pages_now * PAGE)
            step(
                visits,
                lambda h: kv[request, 0, span, pl.ds(h * HD, HD)],
                lambda h: flipped[request, h, :, span],
                None,
                follow,
            )

        def tiles_from(i, together):
            visits = [one_visit(i + j) for j in range(together)]
            if first:
                fresh_visit(*visits[0])
            else:
                for j, (visit, _, _) in enumerate(visits):
                    if follow:
                        state[visit] = backup[i + j]
                    else:
                        backup[i + j] = state[visit]

            def four(j, carry):
                for visit in visits:
                    page_step([visit], 4 * j, 4)
                return carry

            lax.fori_loop(0, n // 4, four, 0)
            for rest in (1, 2, 3):

                @pl.when(n % 4 == rest)
                def _(rest=rest):
                    page_step(visits, (n // 4) * 4, rest)

            if finish or last:
                for visit, row0, _ in visits:
                    complete(visit, row0)

        def fresh_visit(visit, row0, owned):
            key0 = pl.multiple_of((offset // PAGE) * PAGE, PAGE)

            def fresh_step(reach):
                span = pl.ds(key0, reach)
                key = key0 + lax.broadcasted_iota(jnp.int32, (reach, PAGE), 0)
                key = jnp.where(key >= offset, key, blocks + REACH)
                lane = lax.broadcasted_iota(jnp.int32, (reach, PAGE), 1)
                step(
                    [(visit, row0, owned)],
                    lambda h: fresh[0, span, pl.ds(h * HD, HD)],
                    lambda h: fresh_flipped[h, :, span],
                    key <= row0 + lane % TILE,
                    follow,
                )

            near = row0 + TILE - key0 <= REACH // 2

            @pl.when(near)
            def _():
                fresh_step(REACH // 2)

            @pl.when(jnp.logical_not(near))
            def _():
                fresh_step(REACH)

        def complete(visit, row0):
            def put(kept):
                position = row0 + lax.broadcasted_iota(jnp.int32, (kept, 1), 0)
                mine = (position >= offset) & (position < end)
                for h in range(kv_heads):
                    share = state[visit, h, 0:HD, :]
                    share = share * (1.0 / state[visit, h, HD : HD + 1, :])
                    share = jnp.transpose(share.astype(outs.dtype))
                    for g in range(group):
                        columns = pl.ds((h * group + g) * HD, HD)
                        rows = share[g * TILE : (g + 1) * TILE]
                        old = outs[pl.ds(row0, kept), columns].astype(jnp.float32)
                        new = jnp.where(mine, rows[:kept].astype(jnp.float32), old)
                        outs[pl.ds(row0, kept), columns] = new.astype(outs.dtype)
                        if kept < TILE:
                            outs[pl.ds(row0 + kept, TILE - kept), columns] = rows[kept:]

            if finish:

                @pl.when(later[request] == 0)
                def _():
                    put(16)

            else:

                @pl.when(row0 + TILE <= end)
                def _():
                    put(16)

                @pl.when(row0 + TILE > end)
                def _():
                    put(TILE)

        def several(together):
            def body(i, carry):
                tiles_from(i * together, together)
                return carry

            return body

        tiles = visits_of(request)
        if first or follow:
            lax.fori_loop(0, tiles, several(1), 0)
        else:
            lax.fori_loop(0, tiles // 2, several(2), 0)

            @pl.when(tiles % 2 == 1)
            def _():
                tiles_from(tiles - 1, 1)

    def out_copy(c):
        span = pl.ds(pl.multiple_of(c * OUT_CHUNK, OUT_CHUNK), OUT_CHUNK)
        return pltpu.make_async_copy(outs.at[span], result.at[span], out_sems.at[c])

    def out_now(c):
        pending = jnp.bool_(False)
        for request in range(REQ_HOST):
            apart = (info[request, 1] <= c * OUT_CHUNK) | (info[request, 0] >= (c + 1) * OUT_CHUNK)
            again = (later if finish else count)[request] > 0
            pending = pending | (jnp.logical_not(apart) & again)
        return jnp.logical_not(pending) if finish else pending

    def one_request(request, ready):
        ready_rows, ready_out = ready
        if first:
            ready_rows = arrival(request, ready_rows)
        page_arrival(request)
        peak[...] = jnp.zeros_like(peak)
        work(request, False)

        @pl.when(jnp.logical_not(jnp.max(peak[...]) <= LIMIT))
        def _():
            work(request, True)

        if finish or last:
            done = info[request, 1] // 16 * 16 // OUT_CHUNK

            def send(c, carry):
                @pl.when(out_now(c))
                def _():
                    out_copy(c).start()

                return carry

            lax.fori_loop(ready_out, done, send, 0)
            ready_out = done
        return (ready_rows, ready_out)

    lax.fori_loop(0, REQ_HOST, one_request, (jnp.int32(0), jnp.int32(0)))
    if first:
        wait_sends()
    if finish or last:
        for c in range(blocks // OUT_CHUNK):

            @pl.when(out_now(c))
            def _(c=c):
                out_copy(c).wait()


def stage(
    parcels, rest, stores, slots, tables, queries, pages, start, held, finish, last, carried
):
    pieces, codes, others = start
    rows, width = queries.shape
    kv_width = pages[0].shape[3]
    first = held is None
    heads, kv_heads = width // HD, kv_width // HD
    plan = dict(
        parcels=parcels,
        rest=rest,
        stores=stores,
        slots=slots,
        first=first,
        finish=finish,
        last=last,
        rows=rows,
        heads=heads,
        kv_heads=kv_heads,
        pieces=len(pieces),
        carried=len(carried),
        pairs=pairs_of(others),
        others=others,
    )
    visits = (rows + REQ_HOST * (15 + TILE - 1)) // TILE
    most = (MOST_NEW + 15 + TILE - 1) // TILE
    visit_shape = (kv_heads, HD + 16, heads // kv_heads * TILE)
    n_chunks = rows // CHUNK
    scratch = [
        pltpu.VMEM((REQ_HOST, 2, PAGES_MAX * PAGE, kv_width), queries.dtype),
        pltpu.VMEM((REQ_HOST, kv_heads, HD + 16, PAGES_MAX * PAGE), queries.dtype),
        pltpu.VMEM((8, heads // kv_heads // 2 * TILE), jnp.float32),
        pltpu.SMEM((REQ_HOST, 5), jnp.int32),
        pltpu.SMEM((REQ_HOST,), jnp.int32),
        pltpu.SMEM((REQ_HOST,), jnp.int32),
        pltpu.SMEM((REQ_HOST, PAGES_MAX), jnp.int32),
        pltpu.SMEM((stores,), jnp.int32),
        pltpu.SemaphoreType.DMA((REQ_HOST, PAGES_MAX)),
        pltpu.SemaphoreType.DMA((n_chunks,)),
    ]
    if first:
        scratch += [
            pltpu.VMEM((2, rows + REACH, kv_width), queries.dtype),
            pltpu.VMEM((kv_heads, HD + 16, rows + REACH), queries.dtype),
            pltpu.SemaphoreType.DMA((len(pieces),)),
        ] + gather_scratch(others)
    else:
        scratch += [pltpu.VMEM((most,) + visit_shape, jnp.float32)]
    if finish or last:
        scratch += [pltpu.SemaphoreType.DMA((rows // OUT_CHUNK,))]
    operands = list(tables) + [codes[i] for i in pairs_of(others)]
    specs = [SMEM] * len(operands)
    operands += ([in_hbm(queries)] if first else []) + pages + pieces
    specs += [ANY] * (len(operands) - len(specs))
    wide = pltpu.VMEM((rows + TILE, width), queries.dtype)
    out_shape = [pltpu.VMEM((visits,) + visit_shape, jnp.float32), wide]
    if finish or last:
        out_shape += [wide]
    out_specs = [VMEM] * len(out_shape)
    if finish or last:
        out_shape += [jax.ShapeDtypeStruct(queries.shape, queries.dtype)]
        out_specs += [ANY]
    n_held = len(out_shape)
    aliases = {}
    if not first:
        aliases = {len(operands) + i: i for i in range(len(held))}
        operands += list(held)
        specs += out_specs[: len(held)]
    aliases |= {len(operands) + i: len(out_shape) + i for i in range(len(carried))}
    out_specs += [ANY] * (len(carried) + len(others))
    out_shape += [jax.ShapeDtypeStruct(x.shape, x.dtype) for x in carried]
    out_shape += gather_shapes(others, pages[0])
    results = pl.pallas_call(
        functools.partial(stage_kernel, plan),
        out_shape=out_shape,
        in_specs=specs + [ANY] * len(carried),
        out_specs=out_specs,
        scratch_shapes=scratch,
        input_output_aliases=aliases,
        compiler_params=pltpu.CompilerParams(vmem_limit_bytes=VMEM_LIMIT),
        cost_estimate=SMALL,
        name="attend",
    )(*operands, *carried)
    return results[:n_held], results[n_held:]


def swap(values, axis, size, partner):
    return lax.ppermute(values, axis, [(i, i ^ partner) for i in range(size)])


def local(queries, fresh_kv, page_pool, page_host, page_slot, prefix_len, fresh_len):
    stores, tps = lax.axis_size("store"), lax.axis_size("tp")
    slots, head_width = page_pool.shape[0], page_pool.shape[3]
    capacity = max(2, (ENTRIES + stores - 1) // stores)

    partners = list(range(1, stores))
    far = [d for d in partners if d & (stores // 2)]
    near = [d for d in partners if not d & (stores // 2)]
    half = len(far) // 2
    every = tuple(range(capacity))
    near = [(d, every) for d in near]
    early, late = [[(d, every) for d in part] for part in (far[:half], far[half:])]
    cut = max(1, capacity * 3 // 4)
    late, final = [[(d, ranks) for d, _ in late] for ranks in (every[:cut], every[cut:])]

    in_use = jnp.arange(PAGES_MAX, dtype=jnp.int32)[None, :] * PAGE < prefix_len[:, None]
    code = jnp.where(in_use, page_host * slots + page_slot, -1)
    both = jnp.concatenate([code, swap(code, "store", stores, 1)], axis=0)
    codes = [both] + [swap(both, "store", stores, d) for d in range(2, stores, 2)]

    tp_me = lax.axis_index("tp")

    def piece(d):
        return lax.dynamic_slice_in_dim(
            fresh_kv, lax.bitwise_xor(tp_me, jnp.int32(d)) * head_width, head_width, 2
        )

    pieces = [piece(0)] + [swap(piece(d), "tp", tps, d) for d in range(1, tps)]
    def send(parcels, pages):
        return {p: swap(x, "store", stores, p[0]) for p, x in zip(parcels, pages)}

    arrived = send(early + near, collect(early + near, codes, page_pool))

    def attend(parcels, held, carried=(), start=([], [], []), finish=False, last=False):
        pages = [arrived[p] for p in parcels] if held else [in_hbm(page_pool)]
        return stage(
            parcels,
            final if finish else [],
            stores,
            slots,
            (code, prefix_len, fresh_len),
            queries,
            pages,
            start,
            held,
            finish,
            last,
            carried,
        )

    local_pages = [(0, tuple(range(ENTRIES)))]
    held, others = attend(local_pages, None, start=(pieces, codes, late + final))
    arrived |= send(late, others[: len(late)])
    held, others = attend(near, held, others[len(late) :])
    held, others = attend(early, held, others)
    arrived |= send(final, others)
    held, _ = attend(late, held, finish=True)
    held, _ = attend(final, held, last=True)
    return held[-1]


def solution(mesh):
    placed = (
        P("store", "tp"),
        P(None, ("store", "tp"), None),
        P("store", None, None, "tp"),
        P("store", None),
        P("store", None),
        P("store"),
        P("store", None),
    )
    return jax.shard_map(
        local, mesh=mesh, in_specs=placed, out_specs=P("store", "tp"), check_vma=False
    )
```

```python
import functools
import math

import jax
import jax.numpy as jnp
from jax import lax
from jax.experimental import pallas as pl
from jax.experimental.pallas import tpu as pltpu
from jax.sharding import PartitionSpec as P

HD = 128
REQ_HOST = 4
PAGE = 128
PAGES_MAX = 8
MOST_NEW = 384
ENTRIES = REQ_HOST * PAGES_MAX

TILE = 64
REACH = 512
CHUNK = 256
OUT_CHUNK = 128
SCALE = math.log2(math.e) / math.sqrt(HD)
LOW = -3e38
LIMIT = 2.0**60

ANY = pl.BlockSpec(memory_space=pl.ANY)
SMEM = pl.BlockSpec(memory_space=pltpu.SMEM)
VMEM = pl.BlockSpec(memory_space=pltpu.VMEM)
SMALL = pl.CostEstimate(flops=0, bytes_accessed=2**16, transcendentals=0)
VMEM_LIMIT = 24 * 2**20


def in_hbm(values):
    return pltpu.with_memory_space_constraint(values, pltpu.HBM)


def gather(parcels, slots, codes, pool, sends, chosen, sems):
    me = lax.axis_index("store")

    def take(i, rank, slot):
        return pltpu.make_async_copy(pool.at[slot], sends[i].at[rank], sems.at[i, rank])

    for i, (partner, ranks) in enumerate(parcels):
        for rank in range(ranks[-1] + 1):
            chosen[rank] = 0
        table, first_row = codes[partner // 2], REQ_HOST * (partner % 2)

        def scan(entry, found, table=table, first_row=first_row):
            code = table[first_row + entry // PAGES_MAX, entry % PAGES_MAX] - me * slots
            hit = (code >= 0) & (code < slots)
            chosen[found] = jnp.where(hit, code, 0)
            return found + hit.astype(jnp.int32)

        lax.fori_loop(0, ENTRIES, scan, jnp.int32(0), unroll=8)
        for rank in ranks:
            take(i, rank - ranks[0], chosen[rank]).start()

    def wait():
        for i, (_, ranks) in enumerate(parcels):
            for rank in range(len(ranks)):
                take(i, rank, 0).wait()

    return wait


def gather_shapes(parcels, pool):
    return [pltpu.VMEM((len(ranks),) + pool.shape[1:], pool.dtype) for _, ranks in parcels]


def gather_scratch(parcels):
    most = max(ranks[-1] + 1 for _, ranks in parcels)
    return [pltpu.SMEM((most + 2,), jnp.int32), pltpu.SemaphoreType.DMA((len(parcels), most))]


def pairs_of(parcels):
    return sorted({partner // 2 for partner, _ in parcels})


def collect_kernel(parcels, slots, *refs):
    refs = list(refs)
    take_refs = lambda count: [refs.pop(0) for _ in range(count)]
    pairs = pairs_of(parcels)
    codes, (pool,) = dict(zip(pairs, take_refs(len(pairs)))), take_refs(1)
    gather(parcels, slots, codes, pool, take_refs(len(parcels)), *refs)()


def collect(parcels, codes, pool):
    codes = [codes[i] for i in pairs_of(parcels)]
    return pl.pallas_call(
        functools.partial(collect_kernel, parcels, pool.shape[0]),
        out_shape=gather_shapes(parcels, pool),
        in_specs=[SMEM] * len(codes) + [ANY],
        out_specs=[ANY] * len(parcels),
        scratch_shapes=gather_scratch(parcels),
        compiler_params=pltpu.CompilerParams(vmem_limit_bytes=VMEM_LIMIT),
        cost_estimate=SMALL,
        name="collect",
    )(*codes, in_hbm(pool))


def stage_kernel(plan, *refs):
    parcels, first, finish, last = plan["parcels"], plan["first"], plan["finish"], plan["last"]
    blocks, heads, kv_heads = plan["rows"], plan["heads"], plan["kv_heads"]
    group = heads // kv_heads
    most_pages = sum(len(ranks) for _, ranks in parcels)
    refs = list(refs)
    take = lambda n: [refs.pop(0) for _ in range(n)]
    codes, prefix, lengths = take(3)
    if first:
        all_codes = dict(zip(plan["pairs"], take(len(plan["pairs"]))))
        (queries,) = take(1)
    pages = take(len(parcels))
    pieces = take(plan["pieces"]) if first else []
    if not first:
        take(4 if last else 2)
    take(plan["carried"])
    state, q = take(2)
    if finish or last:
        (outs,) = take(1)
    if finish or last:
        (result,) = take(1)
    take(plan["carried"])
    sends = take(len(plan["others"]))
    kv, flipped, peak, info, count, later, valid, counters, page_sems, row_sems = take(10)
    if first:
        fresh, fresh_flipped, fresh_sems = take(3)
        chosen, send_sems = take(2)
    else:
        (backup,) = take(1)
    if finish or last:
        (out_sems,) = take(1)
    me = lax.axis_index("store")
    n_chunks = blocks // CHUNK

    def row_copy(c):
        span = pl.ds(pl.multiple_of(c * CHUNK, CHUNK), CHUNK)
        return pltpu.make_async_copy(queries.at[span], q.at[span], row_sems.at[c])

    offset, base = jnp.int32(0), jnp.int32(0)
    for request in range(REQ_HOST):
        end = offset + lengths[0, request]
        begin_row = (offset // 16) * 16
        tiles = (end - begin_row + TILE - 1) // TILE
        for i, value in enumerate((offset, end, begin_row, tiles, base)):
            info[request, i] = value
        offset, base = end, base + tiles
        count[request] = 0
        later[request] = 0
    for owner in range(plan["stores"]):
        counters[owner] = 0

    def fetch(entry, carry):
        request, page = entry // PAGES_MAX, entry % PAGES_MAX
        code = codes[request, page]
        used = code >= 0
        code = jnp.maximum(code, 0)
        owner, slot = lax.div(code, plan["slots"]), lax.rem(code, plan["slots"])
        rank = counters[owner]
        counters[owner] = rank + used.astype(jnp.int32)
        place = count[request]
        def within(parcel):
            partner, ranks = parcel
            mine = used & (owner == lax.bitwise_xor(me, jnp.int32(partner)))
            return mine & (rank >= ranks[0]) & (rank <= ranks[-1])

        for parcel in plan["rest"]:
            later[request] = later[request] | within(parcel).astype(jnp.int32)
        mine = [within(parcel) for parcel in parcels]

        @pl.when(functools.reduce(jnp.logical_or, mine))
        def _():
            span = pl.ds(pl.multiple_of(place * PAGE, PAGE), PAGE)
            for i, (partner, ranks) in enumerate(parcels):
                index = slot if partner == 0 else rank - ranks[0]

                @pl.when(mine[i])
                def _(i=i, index=index):
                    pltpu.make_async_copy(
                        pages[i].at[index], kv.at[request, :, span], page_sems.at[request, place]
                    ).start()

            valid[request, place] = jnp.minimum(prefix[request] - page * PAGE, PAGE)
            count[request] = place + 1

        return carry

    if first:
        tp_me = lax.axis_index("tp")
        piece_copies = []
        for i in range(len(pieces)):
            n = pieces[i].shape[1]
            span = pl.ds(pl.multiple_of(lax.bitwise_xor(tp_me, jnp.int32(i)) * n, n), n)
            piece_copies.append(pltpu.make_async_copy(pieces[i], fresh.at[:, span], fresh_sems.at[i]))
            piece_copies[-1].start()
        rest = pl.ds(blocks, REACH)
        fresh[0, rest, :] = jnp.zeros((REACH, fresh.shape[2]), fresh.dtype)
        fresh_flipped[:, :, rest] = jnp.zeros((kv_heads, HD + 16, REACH), fresh.dtype)
    if first:
        for c in range(n_chunks):
            row_copy(c).start()
    lax.fori_loop(0, ENTRIES, fetch, 0, unroll=2)
    if first:
        wait_sends = gather(
            plan["others"], plan["slots"], all_codes, pages[0], sends, chosen, send_sems
        )

    part = group // 2
    width = part * TILE
    chains = [(h, c) for h in range(kv_heads) for c in range(2)]

    def flip(values, ones, target, span):
        for h in range(kv_heads):
            part = values[:, h * HD : (h + 1) * HD]
            target[h, 0:HD, span] = jnp.transpose(part.astype(jnp.bfloat16))
            target[h, HD : HD + 16, span] = ones.astype(jnp.bfloat16)

    if first:
        for copy in piece_copies:
            copy.wait()

        def flip_fresh(c, carry):
            span = pl.ds(pl.multiple_of(c * PAGE, PAGE), PAGE)
            flip(
                fresh[1, span, :].astype(jnp.float32),
                jnp.ones((16, PAGE), jnp.float32),
                fresh_flipped,
                span,
            )
            return carry

        lax.fori_loop(0, blocks // PAGE, flip_fresh, 0)

    def step(visits, key_of, value_of, ok, follow):
        begin = ok is not None
        links = [(v, h, c) for v in range(len(visits)) for h, c in chains]
        tops = {}
        if not begin:
            for v, h, c in links:
                tops[v, h, c] = state[visits[v][0], h, HD + 8 : HD + 9, pl.ds(c * width, width)]

        def score(v, h, c):
            rows = pl.ds(visits[v][1], TILE)
            first_head = h * group + c * part
            stacked = jnp.concatenate(
                [q[rows, pl.ds((first_head + g) * HD, HD)] for g in range(part)], axis=0
            )
            scores = lax.dot_general(
                key_of(h), stacked, (((1,), (1,)), ((), ())), preferred_element_type=jnp.float32
            )
            if begin:
                blocks_of = [scores[:, i : i + PAGE] for i in range(0, width, PAGE)]
                scores = jnp.concatenate([jnp.where(ok, x, LOW) for x in blocks_of], axis=1)
            return scores

        def reference(link, scores):
            if begin:
                return jnp.max(scores, axis=0, keepdims=True)
            if follow:
                return jnp.maximum(jnp.max(scores, axis=0, keepdims=True), tops[link])
            return tops[link]

        def update(v, h, c, top, mixed):
            visit, _, owned = visits[v]
            lanes = pl.ds(c * width, width)
            if not begin:
                old = state[visit, h, 0 : HD + 8, lanes]
                if follow:
                    old = old * jnp.exp2((tops[v, h, c] - top) * SCALE)
                mixed = old + mixed
            state[visit, h, 0 : HD + 8, lanes] = mixed
            if begin or follow:
                state[visit, h, HD + 8 : HD + 16, lanes] = jnp.broadcast_to(top, (8, width))
            if not begin and not follow:
                peak[...] = jnp.maximum(peak[...], jnp.where(owned, mixed[HD : HD + 8], 0.0))

        scores = [score(*link) for link in links]
        new_tops = [reference(link, x) for link, x in zip(links, scores)]
        weights = [
            jnp.exp2((x - top) * SCALE).astype(jnp.bfloat16) for x, top in zip(scores, new_tops)
        ]
        mixed = [
            jnp.dot(value_of(link[1]), x, preferred_element_type=jnp.float32)[: HD + 8]
            for link, x in zip(links, weights)
        ]
        for link, top, x in zip(links, new_tops, mixed):
            update(*link, top, x)

    def visits_of(request):
        tiles = info[request, 3]
        return tiles if first or finish else jnp.where(count[request] > 0, tiles, 0)

    def arrival(request, ready_rows):
        end_row = info[request, 2] + visits_of(request) * TILE
        need = jnp.minimum((end_row + CHUNK - 1) // CHUNK, n_chunks)

        def arrive(c, carry):
            row_copy(c).wait()
            return carry

        lax.fori_loop(ready_rows, need, arrive, 0)
        return jnp.maximum(ready_rows, need)

    def page_arrival(request):
        def page_arrive(place, carry):
            span = pl.ds(pl.multiple_of(place * PAGE, PAGE), PAGE)
            pltpu.make_async_copy(
                pages[0].at[0], kv.at[request, :, span], page_sems.at[request, place]
            ).wait()
            here = valid[request, place]
            token = lax.broadcasted_iota(jnp.int32, (PAGE, 1), 0)

            @pl.when(here < PAGE)
            def _():
                keys = kv[request, 0, span, :].astype(jnp.float32)
                kv[request, 0, span, :] = jnp.where(token < here, keys, keys[0:1, :]).astype(kv.dtype)

            values = kv[request, 1, span, :].astype(jnp.float32)
            ones = (lax.broadcasted_iota(jnp.int32, (16, PAGE), 1) < here).astype(jnp.float32)
            flip(jnp.where(token < here, values, 0.0), ones, flipped.at[request], span)
            return carry

        lax.fori_loop(0, count[request], page_arrive, 0)

    def work(request, follow):
        offset, end, begin_row, _, base = [info[request, i] for i in range(5)]
        begin_row = pl.multiple_of(begin_row, 16)
        n = count[request]

        def one_visit(i):
            row0 = pl.multiple_of(begin_row + i * TILE, 16)
            position = row0 + lax.rem(lax.broadcasted_iota(jnp.int32, (1, width), 1), TILE)
            return (base + i, row0, (position >= offset) & (position < end))

        def page_step(visits, place, pages_now):
            span = pl.ds(pl.multiple_of(place * PAGE, PAGE), pages_now * PAGE)
            step(
                visits,
                lambda h: kv[request, 0, span, pl.ds(h * HD, HD)],
                lambda h: flipped[request, h, :, span],
                None,
                follow,
            )

        def tiles_from(i, together):
            visits = [one_visit(i + j) for j in range(together)]
            if first:
                fresh_visit(*visits[0])
            else:
                for j, (visit, _, _) in enumerate(visits):
                    if follow:
                        state[visit] = backup[i + j]
                    else:
                        backup[i + j] = state[visit]

            if follow:

                def single(place, carry):
                    page_step(visits, place, 1)
                    return carry

                lax.fori_loop(0, n, single, 0)
                return

            if most_pages >= 4:

                def four(t, carry):
                    visit = one_visit(i + lax.rem(t, together))
                    page_step([visit], 4 * lax.div(t, together), 4)
                    return carry

                lax.fori_loop(0, n // 4 * together, four, 0)
            for rest in range(1, min(most_pages, 3) + 1):

                @pl.when(n % 4 == rest)
                def _(rest=rest):
                    page_step(visits, (n // 4) * 4, rest)

        def fresh_visit(visit, row0, owned):
            key0 = pl.multiple_of((offset // PAGE) * PAGE, PAGE)

            def fresh_step(reach):
                span = pl.ds(key0, reach)
                key = key0 + lax.broadcasted_iota(jnp.int32, (reach, PAGE), 0)
                key = jnp.where(key >= offset, key, blocks + REACH)
                lane = lax.broadcasted_iota(jnp.int32, (reach, PAGE), 1)
                step(
                    [(visit, row0, owned)],
                    lambda h: fresh[0, span, pl.ds(h * HD, HD)],
                    lambda h: fresh_flipped[h, :, span],
                    key <= row0 + lane % TILE,
                    follow,
                )

            near = row0 + TILE - key0 <= REACH // 2

            @pl.when(near)
            def _():
                fresh_step(REACH // 2)

            @pl.when(jnp.logical_not(near))
            def _():
                fresh_step(REACH)

        def complete(visit, row0):
            def put(kept):
                position = row0 + lax.broadcasted_iota(jnp.int32, (kept, 1), 0)
                mine = (position >= offset) & (position < end)
                for h in range(kv_heads):
                    share = state[visit, h, 0:HD, :]
                    share = share * (1.0 / state[visit, h, HD : HD + 1, :])
                    share = jnp.transpose(share.astype(outs.dtype))
                    for g in range(group):
                        columns = pl.ds((h * group + g) * HD, HD)
                        rows = share[g * TILE : (g + 1) * TILE]
                        old = outs[pl.ds(row0, kept), columns].astype(jnp.float32)
                        new = jnp.where(mine, rows[:kept].astype(jnp.float32), old)
                        outs[pl.ds(row0, kept), columns] = new.astype(outs.dtype)
                        if kept < TILE:
                            outs[pl.ds(row0 + kept, TILE - kept), columns] = rows[kept:]

            if finish:

                @pl.when(later[request] == 0)
                def _():
                    put(16)

            else:

                @pl.when(row0 + TILE <= end)
                def _():
                    put(16)

                @pl.when(row0 + TILE > end)
                def _():
                    put(TILE)

        def several(together):
            def body(i, carry):
                tiles_from(i * together, together)
                return carry

            return body

        def complete_one(i, carry):
            visit, row0, _ = one_visit(i)
            complete(visit, row0)
            return carry

        tiles = visits_of(request)
        if first or follow:
            lax.fori_loop(0, tiles, several(1), 0)
        else:
            lax.fori_loop(0, tiles // 2, several(2), 0)

            @pl.when(tiles % 2 == 1)
            def _():
                tiles_from(tiles - 1, 1)

        if finish or last:
            lax.fori_loop(0, tiles, complete_one, 0)

    def out_copy(c):
        span = pl.ds(pl.multiple_of(c * OUT_CHUNK, OUT_CHUNK), OUT_CHUNK)
        return pltpu.make_async_copy(outs.at[span], result.at[span], out_sems.at[c])

    def out_now(c):
        pending = jnp.bool_(False)
        for request in range(REQ_HOST):
            apart = (info[request, 1] <= c * OUT_CHUNK) | (info[request, 0] >= (c + 1) * OUT_CHUNK)
            again = (later if finish else count)[request] > 0
            pending = pending | (jnp.logical_not(apart) & again)
        return jnp.logical_not(pending) if finish else pending

    def one_request(request, ready):
        ready_rows, ready_out = ready
        if first:
            ready_rows = arrival(request, ready_rows)
        page_arrival(request)
        peak[...] = jnp.zeros_like(peak)
        work(request, False)

        @pl.when(jnp.logical_not(jnp.max(peak[...]) <= LIMIT))
        def _():
            work(request, True)

        if finish or last:
            done = info[request, 1] // 16 * 16 // OUT_CHUNK

            def send(c, carry):
                @pl.when(out_now(c))
                def _():
                    out_copy(c).start()

                return carry

            lax.fori_loop(ready_out, done, send, 0)
            ready_out = done
        return (ready_rows, ready_out)

    lax.fori_loop(0, REQ_HOST, one_request, (jnp.int32(0), jnp.int32(0)))
    if first:
        wait_sends()
    if finish or last:
        for c in range(blocks // OUT_CHUNK):

            @pl.when(out_now(c))
            def _(c=c):
                out_copy(c).wait()


def stage(
    parcels, rest, stores, slots, tables, queries, pages, start, held, finish, last, carried
):
    pieces, codes, others = start
    rows, width = queries.shape
    kv_width = pages[0].shape[3]
    first = held is None
    heads, kv_heads = width // HD, kv_width // HD
    plan = dict(
        parcels=parcels,
        rest=rest,
        stores=stores,
        slots=slots,
        first=first,
        finish=finish,
        last=last,
        rows=rows,
        heads=heads,
        kv_heads=kv_heads,
        pieces=len(pieces),
        carried=len(carried),
        pairs=pairs_of(others),
        others=others,
    )
    visits = (rows + REQ_HOST * (15 + TILE - 1)) // TILE
    most = (MOST_NEW + 15 + TILE - 1) // TILE
    visit_shape = (kv_heads, HD + 16, heads // kv_heads * TILE)
    n_chunks = rows // CHUNK
    scratch = [
        pltpu.VMEM((REQ_HOST, 2, PAGES_MAX * PAGE, kv_width), queries.dtype),
        pltpu.VMEM((REQ_HOST, kv_heads, HD + 16, PAGES_MAX * PAGE), queries.dtype),
        pltpu.VMEM((8, heads // kv_heads // 2 * TILE), jnp.float32),
        pltpu.SMEM((REQ_HOST, 5), jnp.int32),
        pltpu.SMEM((REQ_HOST,), jnp.int32),
        pltpu.SMEM((REQ_HOST,), jnp.int32),
        pltpu.SMEM((REQ_HOST, PAGES_MAX), jnp.int32),
        pltpu.SMEM((stores,), jnp.int32),
        pltpu.SemaphoreType.DMA((REQ_HOST, PAGES_MAX)),
        pltpu.SemaphoreType.DMA((n_chunks,)),
    ]
    if first:
        scratch += [
            pltpu.VMEM((2, rows + REACH, kv_width), queries.dtype),
            pltpu.VMEM((kv_heads, HD + 16, rows + REACH), queries.dtype),
            pltpu.SemaphoreType.DMA((len(pieces),)),
        ] + gather_scratch(others)
    else:
        scratch += [pltpu.VMEM((most,) + visit_shape, jnp.float32)]
    if finish or last:
        scratch += [pltpu.SemaphoreType.DMA((rows // OUT_CHUNK,))]
    operands = list(tables) + [codes[i] for i in pairs_of(others)]
    specs = [SMEM] * len(operands)
    operands += ([in_hbm(queries)] if first else []) + pages + pieces
    specs += [ANY] * (len(operands) - len(specs))
    wide = pltpu.VMEM((rows + TILE, width), queries.dtype)
    out_shape = [pltpu.VMEM((visits,) + visit_shape, jnp.float32), wide]
    if finish or last:
        out_shape += [wide]
    out_specs = [VMEM] * len(out_shape)
    if finish or last:
        out_shape += [jax.ShapeDtypeStruct(queries.shape, queries.dtype)]
        out_specs += [ANY]
    n_held = len(out_shape)
    aliases = {}
    if not first:
        aliases = {len(operands) + i: i for i in range(len(held))}
        operands += list(held)
        specs += out_specs[: len(held)]
    aliases |= {len(operands) + i: len(out_shape) + i for i in range(len(carried))}
    out_specs += [ANY] * (len(carried) + len(others))
    out_shape += [jax.ShapeDtypeStruct(x.shape, x.dtype) for x in carried]
    out_shape += gather_shapes(others, pages[0])
    results = pl.pallas_call(
        functools.partial(stage_kernel, plan),
        out_shape=out_shape,
        in_specs=specs + [ANY] * len(carried),
        out_specs=out_specs,
        scratch_shapes=scratch,
        input_output_aliases=aliases,
        compiler_params=pltpu.CompilerParams(vmem_limit_bytes=VMEM_LIMIT),
        cost_estimate=SMALL,
        name="attend",
    )(*operands, *carried)
    return results[:n_held], results[n_held:]


def swap(values, axis, size, partner):
    return lax.ppermute(values, axis, [(i, i ^ partner) for i in range(size)])


def local(queries, fresh_kv, page_pool, page_host, page_slot, prefix_len, fresh_len):
    stores, tps = lax.axis_size("store"), lax.axis_size("tp")
    slots, head_width = page_pool.shape[0], page_pool.shape[3]
    capacity = max(2, (ENTRIES + stores - 1) // stores)

    partners = list(range(1, stores))
    far = [d for d in partners if d & (stores // 2)]
    near = [d for d in partners if not d & (stores // 2)]
    half = len(far) // 2
    every = tuple(range(capacity))
    near = [(d, every) for d in near]
    early, late = [[(d, every) for d in part] for part in (far[:half], far[half:])]
    cut = max(1, capacity * 3 // 4)
    late, final = [[(d, ranks) for d, _ in late] for ranks in (every[:cut], every[cut:])]

    in_use = jnp.arange(PAGES_MAX, dtype=jnp.int32)[None, :] * PAGE < prefix_len[:, None]
    code = jnp.where(in_use, page_host * slots + page_slot, -1)
    both = jnp.concatenate([code, swap(code, "store", stores, 1)], axis=0)
    codes = [both] + [swap(both, "store", stores, d) for d in range(2, stores, 2)]

    tp_me = lax.axis_index("tp")

    def piece(d):
        return lax.dynamic_slice_in_dim(
            fresh_kv, lax.bitwise_xor(tp_me, jnp.int32(d)) * head_width, head_width, 2
        )

    pieces = [piece(0)] + [swap(piece(d), "tp", tps, d) for d in range(1, tps)]
    def send(parcels, pages):
        return {p: swap(x, "store", stores, p[0]) for p, x in zip(parcels, pages)}

    arrived = send(early + near, collect(early + near, codes, page_pool))

    def attend(parcels, held, carried=(), start=([], [], []), finish=False, last=False):
        pages = [arrived[p] for p in parcels] if held else [in_hbm(page_pool)]
        return stage(
            parcels,
            final if finish else [],
            stores,
            slots,
            (code, prefix_len, fresh_len),
            queries,
            pages,
            start,
            held,
            finish,
            last,
            carried,
        )

    local_pages = [(0, tuple(range(ENTRIES)))]
    held, others = attend(local_pages, None, start=(pieces, codes, late + final))
    arrived |= send(late, others[: len(late)])
    held, others = attend(near, held, others[len(late) :])
    held, others = attend(early, held, others)
    arrived |= send(final, others)
    held, _ = attend(late, held, finish=True)
    held, _ = attend(final, held, last=True)
    return held[-1]


def solution(mesh):
    placed = (
        P("store", "tp"),
        P(None, ("store", "tp"), None),
        P("store", None, None, "tp"),
        P("store", None),
        P("store", None),
        P("store"),
        P("store", None),
    )
    return jax.shard_map(
        local, mesh=mesh, in_specs=placed, out_specs=P("store", "tp"), check_vma=False
    )
```
